32 devices in a mesh: tgt: 4 (over z), src: 8 (over y, x, core).
Axes of the slice: x: 2, y: 2, z: 4, core: 2. Of those that a mesh axis runs over, the one named last changes fastest.
Arguments:
- vol_grad: float32 [128, 16384], P(None, ('tgt', 'src')), may hold values from -6 to 6
- vol_coords: float32 [3, 16384], P(None, ('tgt', 'src')), may hold values from 0 to 1
- ctrl_coords: float32 [3, 8192], P(None, ('tgt', 'src')), may hold values from 0 to 1
Outputs:
- adjoint_controls: float32 [128, 8192], P(None, ('tgt', 'src'))
The draws below stay inside these ranges and needn't reach their ends.
All inputs are finite; a program needn't handle non-finite values.
Results may differ from the reference program's by a relative error of at most 0.0003.
Values sent between devices are 32-bit elements; how exact they have to be, the bound alone decides.
No kernel may reach another device: no remote copies, remote signals or barrier semaphores. Data moves between devices by JAX's collectives and lax.ppermute only.
A program may use at most 64 MiB of HBM per device.

```python
import math
import jax
import jax.numpy as jnp
from jax import lax

G = 128
STEPS = 2
VOLUME = 16384
CONTROLS = 8192


def level_of(key, dims, split, smallest, largest):
    def one(axis_at, parts):
        heights = jax.random.uniform(jax.random.fold_in(jax.random.fold_in(key, 6), axis_at), (parts,), jnp.float32, smallest / len(split), largest / len(split))
        return jnp.repeat(jnp.exp(heights), dims[axis_at] // parts).reshape((-1,) + (1,) * (len(dims) - axis_at - 1))

    level = one(*split[0])
    for cut in split[1:]:
        level = level * one(*cut)
    return level


def normal_values(stream_key, shape, scale, most, cuts=(), kind=jnp.bfloat16):
    gain = level_of(stream_key, shape, cuts, -0.22, 0.18) if cuts else 1.0
    array = jax.random.normal(stream_key, shape, jnp.float32) * scale * gain
    return jnp.minimum(jnp.maximum(array, -most), most).astype(kind)


def setup_inputs(seed: int = 0) -> dict:
    key_of = jax.random.split(jax.random.key(seed), 4)
    return {
        "vol_grad": normal_values(key_of[0], (G, VOLUME), 1.0, 6.0, ((1, 32),), jnp.float32),
        "vol_coords": jnp.clip(1.0 * jax.random.uniform(key_of[1], (3, VOLUME), jnp.float32) ** level_of(key_of[1], (3, VOLUME), ((1, 32),), -0.2, 0.2), 0.0, 1.0),
        "ctrl_coords": jnp.clip(1.0 * jax.random.uniform(key_of[2], (3, CONTROLS), jnp.float32) ** level_of(key_of[2], (3, CONTROLS), ((1, 32),), -0.2, 0.2), 0.0, 1.0),
    }


neighbours = 64.0
ridge_term = 1.0
omegas = [1.0 / (0.55 + 0.45 * math.cos(math.pi * (2 * k + 1) / 4.0)) for k in range(2)]

def wendland(sources, targets, radius):
    delta_x = sources[0][:, None] - targets[0][None, :]
    delta_y = sources[1][:, None] - targets[1][None, :]
    delta_z = sources[2][:, None] - targets[2][None, :]
    distance = jnp.sqrt(delta_x * delta_x + delta_y * delta_y + delta_z * delta_z)
    falloff = jnp.maximum(1.0 - distance / radius, 0.0)
    square = falloff * falloff
    return square * square * (4.0 * distance / radius + 1.0)

def contract(sources, vectors, targets, radius):
    length_in = sources.shape[1]
    block_len = math.gcd(length_in, 512)
    blocks = length_in // block_len
    width = targets.shape[1]

    def add(which, state_pair):
        accum, column_sums = state_pair
        chosen = lax.dynamic_slice_in_dim(sources, which * block_len, block_len, 1)
        values = lax.dynamic_slice_in_dim(vectors, which * block_len, block_len, 1)
        kernel_tile = wendland(chosen, targets, radius)
        accum = accum + jnp.dot(values, kernel_tile, precision=lax.Precision.HIGHEST, preferred_element_type=jnp.float32)
        column_sums = column_sums + lax.optimization_barrier(jnp.sum(kernel_tile, axis=0, keepdims=True))
        return (accum, column_sums)
    start = (jnp.zeros((vectors.shape[0], width), jnp.float32), jnp.zeros((1, width), jnp.float32))
    return lax.fori_loop(0, blocks, add, start)

def reference(vol_grad, vol_coords, ctrl_coords):
    radius = (3.0 * neighbours / (4.0 * math.pi * CONTROLS)) ** (1.0 / 3.0)
    pullback, unused = contract(vol_coords, vol_grad, ctrl_coords, radius)
    iterate = pullback
    for sweep in range(STEPS):
        product, column_sums = contract(ctrl_coords, iterate, ctrl_coords, radius)
        scaling = 1.0 / (column_sums + ridge_term)
        iterate = iterate + omegas[sweep] * scaling * (pullback - product - iterate)
    return iterate
```

```python
import functools
import math

import jax
import jax.numpy as jnp
from jax import lax
from jax.experimental import pallas as pl
from jax.experimental.pallas import tpu as pltpu
from jax.sharding import PartitionSpec as P

STEPS = 2
COORDS = 8
FEATURES = 32
ONES = 16
KEPT_BYTES = 20 << 20

neighbours = 64.0
ridge_term = 1.0
omegas = [1.0 / (0.55 + 0.45 * math.cos(math.pi * (2 * k + 1) / 4.0)) for k in range(2)]

BF16 = jnp.bfloat16
F32 = jnp.float32


def parts_of(value, count):
    terms = []
    for _ in range(count):
        term = value.astype(BF16)
        terms.append(term)
        value = value - term.astype(F32)
    return terms


def point_features(points, inverse, as_rows):
    scaled = (points - 0.5) * inverse
    axes = [scaled[d : d + 1] for d in range(3)]
    norm = parts_of(axes[0] * axes[0] + axes[1] * axes[1] + axes[2] * axes[2], 3)
    one = jnp.ones_like(norm[0])
    found = []
    for axis in axes:
        if as_rows:
            a, b, c = parts_of(-2.0 * axis, 3)
            found += [a, a, b, b, a, c]
        else:
            a, b, c = parts_of(axis, 3)
            found += [a, b, a, b, c, a]
    found += norm + [one] * 3 if as_rows else [one] * 3 + norm
    found += [jnp.zeros_like(one)] * (FEATURES - len(found))
    return jnp.concatenate([f.astype(F32) for f in found], axis=0).astype(BF16)


def quarter_wendland(square):
    square = jnp.minimum(jnp.maximum(square, 1e-12), 1.0)
    distance = square * lax.rsqrt(square)
    falloff = 1.0 - distance
    falloff = falloff * falloff
    return (falloff * falloff) * (distance + 0.25)


def evaluate(rows, row_start, cols, high, low, high_start, sub):
    count, width = rows.shape[1], cols.shape[1]
    for at in range(0, count, sub):
        square = lax.dot_general(
            rows[:, at : at + sub], cols, (((0,), (0,)), ((), ())), preferred_element_type=F32
        )
        value = quarter_wendland(square)
        rounded = value.astype(BF16)
        high[row_start + at : row_start + at + sub, high_start : high_start + width] = rounded
        low[row_start + at : row_start + at + sub, high_start : high_start + width] = (
            value - rounded.astype(F32)
        ).astype(BF16)


def product(stacked, half, high, low):
    coarse = jnp.dot(stacked, high, preferred_element_type=F32)
    fine = jnp.dot(stacked[:half], low, preferred_element_type=F32)
    return coarse, fine


def pull_kernel(inverse, half, peers, first, *refs):
    refs = list(refs)
    block = refs.pop(0)
    if first:
        ctrl = [refs.pop(0) for _ in range(peers)]
    else:
        given = refs.pop(0)
        before = [refs.pop(0) for _ in range(peers)]
    if first:
        cols = refs.pop(0)
    after = [refs.pop(0) for _ in range(peers)]
    stacked, rows, high, low = refs
    width = after[0].shape[1]
    a, b = parts_of(block[:half] * 4.0, 2)
    stacked[:half] = a
    stacked[half:] = b
    rows[...] = point_features(block[half : half + 3], inverse, True)
    if first:
        for k in range(peers):
            cols[:, k * width : (k + 1) * width] = point_features(ctrl[k][...], inverse, False)
    else:
        cols = given
    step = 2 if peers % 2 == 0 else 1
    for k in range(0, peers, step):
        evaluate(rows, 0, cols[:, k * width : (k + step) * width], high, low, 0, 128)
        coarse, fine = product(stacked[...], half, high[...], low[...])
        total = coarse[:half] + coarse[half:] + fine
        for i in range(step):
            part = total[:, i * width : (i + 1) * width]
            after[k + i][...] = part if first else before[k + i][...] + part


def keep_kernel(inverse, peers, *refs):
    coords, cols, high, low, rows = refs[:peers], refs[peers], refs[peers + 1], refs[peers + 2], refs[peers + 3]
    count = coords[0].shape[1]
    width = 512 if cols.shape[1] % 512 == 0 else cols.shape[1]
    for k in range(peers):
        rows[...] = point_features(coords[k][3:6], inverse, True)
        for at in range(0, cols.shape[1], width):
            evaluate(rows, k * count, cols[:, at : at + width], high, low, at, 128)


def step_kernel(half, peers, with_sums, *refs):
    blocks, high, low = refs[:peers], refs[peers], refs[peers + 1]
    outs, stacked = refs[peers + 2 : 2 * peers + 2], refs[2 * peers + 2]
    count = blocks[0].shape[1]
    upper = half + (ONES if with_sums else 0)
    for k in range(peers):
        a, b = parts_of(blocks[k][...] * 4.0, 2)
        stacked[:half, k * count : (k + 1) * count] = a
        stacked[upper:, k * count : (k + 1) * count] = b
    if with_sums:
        stacked[half:upper, :] = jnp.full((ONES, stacked.shape[1]), 4.0, BF16)
    step = 2 if peers % 2 == 0 else 1
    for k in range(0, peers, step):
        span = slice(k * count, (k + step) * count)
        coarse, fine = product(stacked[...], upper, high[:, span], low[:, span])
        total = coarse[:half] + coarse[upper:] + fine[:half]
        for i in range(step):
            at = slice(i * count, (i + 1) * count)
            outs[k + i][:half] = total[:, at]
            if with_sums:
                outs[k + i][half:] = coarse[half : half + 8, at] + fine[half : half + 8, at]


def again_kernel(inverse, half, peers, with_sums, *refs):
    blocks, coords, cols = refs[:peers], refs[peers : 2 * peers], refs[2 * peers]
    outs = refs[2 * peers + 1 : 3 * peers + 1]
    stacked, rows, high, low = refs[3 * peers + 1 :]
    count = blocks[0].shape[1]
    upper = half + (ONES if with_sums else 0)
    if with_sums:
        stacked[half:upper, :] = jnp.full((ONES, count), 4.0, BF16)
    for k in range(peers):
        a, b = parts_of(blocks[k][...] * 4.0, 2)
        stacked[:half] = a
        stacked[upper:] = b
        rows[...] = point_features(coords[k][3:6], inverse, True)
        for j in range(peers):
            evaluate(rows, 0, cols[:, j * count : (j + 1) * count], high, low, 0, 128)
            coarse, fine = product(stacked[...], upper, high[...], low[...])
            total = coarse[:half] + coarse[upper:] + fine[:half]
            outs[j][:half] = total if k == 0 else outs[j][:half] + total
            if with_sums:
                sums = coarse[half : half + 8] + fine[half : half + 8]
                outs[j][half:] = sums if k == 0 else outs[j][half:] + sums


def vmem(count):
    return [pl.BlockSpec(memory_space=pltpu.VMEM)] * count


def params():
    return pltpu.CompilerParams(vmem_limit_bytes=24 << 20)


def cost(rows, cols, half, evaluated):
    return pl.CostEstimate(
        flops=rows * cols * (6 * half + (200 if evaluated else 0)), bytes_accessed=4 * rows * half, transcendentals=0
    )


def per_device(vol_grad, vol_coords, ctrl_coords):
    tgt, src = lax.axis_size("tgt"), lax.axis_size("src")
    chips = src // 2
    peers = tgt
    if chips != tgt or src % 2 or tgt & (tgt - 1):
        raise ValueError("unsupported mesh")
    half = vol_grad.shape[0] // 2
    volume, owned = vol_grad.shape[1], ctrl_coords.shape[1]
    overall = owned * tgt * src
    radius = (3.0 * neighbours / (4.0 * math.pi * overall)) ** (1.0 / 3.0)
    inverse = 1.0 / radius
    core = lax.axis_index("src") % 2
    first_core = core == 0

    sibling = [(i, i ^ 1) for i in range(src)]

    def moved(flip, gather):
        pairs = []
        for t in range(tgt):
            for c in range(chips):
                for r in range(2):
                    along_src = (r == 0) == gather
                    to_t, to_c = (t, c ^ flip) if along_src else (t ^ flip, c)
                    pairs.append(((t * chips + c) * 2 + r, (to_t * chips + to_c) * 2 + r))
        return pairs

    gather_pairs = [moved(k, True) for k in range(peers)]
    sum_pairs = [moved(k, False) for k in range(peers)]

    def exchange(value, pairs):
        return lax.ppermute(value, ("tgt", "src"), pairs)

    mine = jnp.where(first_core, vol_grad[:half], vol_grad[half:])
    other = jnp.where(first_core, vol_grad[half:], vol_grad[:half])
    coords = jnp.concatenate(
        [vol_coords, jnp.pad(ctrl_coords, ((0, 0), (0, volume - owned))), jnp.zeros((2, volume), F32)], axis=0
    )
    got = lax.ppermute(jnp.concatenate([other, coords], axis=0), "src", sibling)
    ctrl = jnp.concatenate([ctrl_coords, got[half + 3 : half + 6, :owned]], axis=1)
    chip_coords = jnp.concatenate(
        [
            jnp.concatenate([vol_coords, got[half : half + 3]], axis=1),
            jnp.pad(ctrl, ((0, 0), (0, 2 * (volume - owned)))),
            jnp.zeros((2, 2 * volume), F32),
        ],
        axis=0,
    )
    block = jnp.concatenate([jnp.concatenate([mine, got[:half]], axis=1), chip_coords], axis=0)

    col_ctrl = [ctrl] + [exchange(ctrl, sum_pairs[k]) for k in range(1, peers)]
    blocks = [block] + [exchange(block, gather_pairs[k]) for k in range(1, peers)]

    width = 2 * owned
    cols_shape = jax.ShapeDtypeStruct((FEATURES, peers * width), BF16)
    partial_shapes = [jax.ShapeDtypeStruct((half, width), F32)] * peers
    step = 2 if peers % 2 == 0 else 1
    pull_scratch = [
        pltpu.VMEM((2 * half, 2 * volume), BF16),
        pltpu.VMEM((FEATURES, 2 * volume), BF16),
        pltpu.VMEM((2 * volume, step * width), BF16),
        pltpu.VMEM((2 * volume, step * width), BF16),
    ]
    found = pl.pallas_call(
        functools.partial(pull_kernel, inverse, half, peers, True),
        out_shape=[cols_shape] + partial_shapes,
        in_specs=vmem(1 + peers),
        out_specs=vmem(1 + peers),
        scratch_shapes=pull_scratch,
        compiler_params=params(),
        cost_estimate=cost(2 * volume, peers * width, half, True),
    )(block, *col_ctrl)
    cols, partials = found[0], found[1:]
    for k in range(1, peers):
        partials = pl.pallas_call(
            functools.partial(pull_kernel, inverse, half, peers, False),
            out_shape=partial_shapes,
            in_specs=vmem(2 + peers),
            out_specs=vmem(peers),
            scratch_shapes=pull_scratch,
            input_output_aliases={2 + i: i for i in range(peers)},
            compiler_params=params(),
            cost_estimate=cost(2 * volume, peers * width, half, True),
        )(blocks[k], cols, *partials)

    def summed(values):
        total = values[0]
        for k in range(1, peers):
            total = total + exchange(values[k], sum_pairs[k])
        return total

    pullback = summed(partials)

    kept = (peers * width) ** 2 * 4 <= KEPT_BYTES
    coords_spec = [pl.BlockSpec((COORDS, width), lambda _: (half // COORDS, 0))] * peers
    if kept:
        high, low = pl.pallas_call(
            functools.partial(keep_kernel, inverse, peers),
            grid=(1,),
            out_shape=[pltpu.VMEM((peers * width, peers * width), BF16)] * 2,
            in_specs=coords_spec + vmem(1),
            out_specs=vmem(2),
            scratch_shapes=[pltpu.VMEM((FEATURES, width), BF16)],
            compiler_params=params(),
            cost_estimate=cost(peers * width, peers * width, 0, True),
        )(*blocks, cols)

    iterate = pullback
    for sweep in range(STEPS):
        arrived = [iterate] + [exchange(iterate, gather_pairs[k]) for k in range(1, peers)]
        with_sums = sweep == 0
        upper = half + (ONES if with_sums else 0)
        out_rows = half + (8 if with_sums else 0)
        out_shape = [jax.ShapeDtypeStruct((out_rows, width), F32)] * peers
        if kept:
            products = pl.pallas_call(
                functools.partial(step_kernel, half, peers, with_sums),
                out_shape=out_shape,
                in_specs=vmem(peers + 2),
                out_specs=vmem(peers),
                scratch_shapes=[pltpu.VMEM((upper + half, peers * width), BF16)],
                compiler_params=params(),
                cost_estimate=cost(peers * width, peers * width, half, False),
            )(
                *arrived,
                pltpu.with_memory_space_constraint(high, pltpu.VMEM),
                pltpu.with_memory_space_constraint(low, pltpu.VMEM),
            )
        else:
            products = pl.pallas_call(
                functools.partial(again_kernel, inverse, half, peers, with_sums),
                grid=(1,),
                out_shape=out_shape,
                in_specs=vmem(peers) + coords_spec + vmem(1),
                out_specs=vmem(peers),
                scratch_shapes=[
                    pltpu.VMEM((upper + half, width), BF16),
                    pltpu.VMEM((FEATURES, width), BF16),
                    pltpu.VMEM((width, width), BF16),
                    pltpu.VMEM((width, width), BF16),
                ],
                compiler_params=params(),
                cost_estimate=cost(peers * width, peers * width, half, True),
            )(*arrived, *blocks, cols)
        total = summed(products)
        if with_sums:
            scaling = 1.0 / (total[half : half + 1] + ridge_term)
        iterate = iterate + omegas[sweep] * scaling * (pullback - total[:half] - iterate)

    own, theirs = iterate[:, :owned], iterate[:, owned:]
    back = lax.ppermute(theirs, "src", sibling)
    return jnp.where(
        first_core, jnp.concatenate([own, back], axis=0), jnp.concatenate([back, own], axis=0)
    )


def solution(mesh):
    placed = (P(None, ("tgt", "src")), P(None, ("tgt", "src")), P(None, ("tgt", "src")))
    return jax.shard_map(
        per_device, mesh=mesh, in_specs=placed, out_specs=P(None, ("tgt", "src")), check_vma=False
    )
```

```python
import functools
import math

import jax
import jax.numpy as jnp
from jax import lax
from jax.experimental import pallas as pl
from jax.experimental.pallas import tpu as pltpu
from jax.sharding import PartitionSpec as P

STEPS = 2
COORDS = 8
FEATURES = 32
ONES = 16
KEPT_BYTES = 20 << 20

neighbours = 64.0
ridge_term = 1.0
omegas = [1.0 / (0.55 + 0.45 * math.cos(math.pi * (2 * k + 1) / 4.0)) for k in range(2)]

BF16 = jnp.bfloat16
F32 = jnp.float32


def parts_of(value, count):
    terms = []
    for _ in range(count):
        term = value.astype(BF16)
        terms.append(term)
        value = value - term.astype(F32)
    return terms


def point_features(points, inverse, as_rows):
    scaled = (points - 0.5) * inverse
    axes = [scaled[d : d + 1] for d in range(3)]
    norm = parts_of(axes[0] * axes[0] + axes[1] * axes[1] + axes[2] * axes[2], 3)
    one = jnp.ones_like(norm[0])
    found = []
    for axis in axes:
        if as_rows:
            a, b, c = parts_of(-2.0 * axis, 3)
            found += [a, a, b, b, a, c]
        else:
            a, b, c = parts_of(axis, 3)
            found += [a, b, a, b, c, a]
    found += norm + [one] * 3 if as_rows else [one] * 3 + norm
    found += [jnp.zeros_like(one)] * (FEATURES - len(found))
    return jnp.concatenate([f.astype(F32) for f in found], axis=0).astype(BF16)


def quarter_wendland(square):
    square = jnp.minimum(jnp.maximum(square, 1e-12), 1.0)
    distance = square * lax.rsqrt(square)
    falloff = 1.0 - distance
    falloff = falloff * falloff
    return (falloff * falloff) * (distance + 0.25)


def evaluate(rows, row_start, cols, high, low, high_start, sub):
    count, width = rows.shape[1], cols.shape[1]
    for at in range(0, count, sub):
        square = lax.dot_general(
            rows[:, at : at + sub], cols, (((0,), (0,)), ((), ())), preferred_element_type=F32
        )
        value = quarter_wendland(square)
        rounded = value.astype(BF16)
        high[row_start + at : row_start + at + sub, high_start : high_start + width] = rounded
        low[row_start + at : row_start + at + sub, high_start : high_start + width] = (
            value - rounded.astype(F32)
        ).astype(BF16)


def product(stacked, half, high, low):
    coarse = jnp.dot(stacked, high, preferred_element_type=F32)
    fine = jnp.dot(stacked[:half], low, preferred_element_type=F32)
    return coarse, fine


def pull_kernel(inverse, full, spans, first, last, *refs):
    refs = list(refs)
    core = refs.pop(0)
    block = refs.pop(0)
    if first:
        sources = [refs.pop(0) for _ in spans]
        cols, after = refs.pop(0), refs.pop(0)
    else:
        cols, before = refs.pop(0), refs.pop(0)
        after = [refs.pop(0) for _ in range(len(spans) + 1)] if last else refs.pop(0)
    stacked, rows, high, low = refs
    half, width = full // 2, cols.shape[1] // (len(spans) * (2 if last else 1))
    a, b = parts_of(block[:full] * 4.0, 2)
    stacked[:full] = a
    stacked[full:] = b
    rows[...] = point_features(block[full : full + 3], inverse, True)
    if first:
        for k in spans:
            cols[:, k * width : (k + 1) * width] = point_features(sources[k][...], inverse, False)
    step = 2 if len(spans) % 2 == 0 else 1
    for k in range(0, len(spans), step):
        at = slice(spans[k] * width, (spans[k] + step) * width)
        evaluate(rows, 0, cols[:, at], high, low, 0, 128)
        coarse, fine = product(stacked[...], full, high[...], low[...])
        total = coarse[:full] + coarse[full:] + fine
        if not first:
            total = before[:, at] + total
        if not last:
            after[:, at] = total
            continue
        mine = jnp.where(core[0] == 0, total[:half], total[half:])
        for i in range(step):
            after[k + i][...] = mine[:, i * width : (i + 1) * width]
        after[-1][:, k * width : (k + step) * width] = jnp.where(core[0] == 0, total[half:], total[:half])


def keep_kernel(inverse, row_points, col_points, high, low, zero, rows, cols):
    zero[...] = jnp.zeros_like(zero)
    rows[...] = point_features(row_points[...], inverse, True)
    cols[...] = point_features(col_points[...], inverse, False)
    count, width = rows.shape[1], math.gcd(cols.shape[1], 1024)

    def tile(which, carry):
        at = pl.ds(pl.multiple_of(which * width, width), width)
        wide = cols[:, at]
        for row in range(0, count, 256):
            square = lax.dot_general(
                rows[:, row : row + 256], wide, (((0,), (0,)), ((), ())), preferred_element_type=F32
            )
            value = quarter_wendland(square)
            rounded = value.astype(BF16)
            high[row : row + 256, at] = rounded
            low[row : row + 256, at] = (value - rounded.astype(F32)).astype(BF16)
        return carry

    lax.fori_loop(0, cols.shape[1] // width, tile, 0)


def step_kernel(half, peers, spans, with_sums, *refs):
    blocks, high, low = refs[:peers], refs[peers], refs[peers + 1]
    outs, stacked = refs[peers + 2 : -1], refs[-1]
    count = blocks[0].shape[1]
    upper = half + (ONES if with_sums else 0)
    for k in range(peers):
        a, b = parts_of(blocks[k][...] * 4.0, 2)
        stacked[:half, k * count : (k + 1) * count] = a
        stacked[upper:, k * count : (k + 1) * count] = b
    if with_sums:
        stacked[half:upper, :] = jnp.full((ONES, stacked.shape[1]), 4.0, BF16)
    step = 2 if len(spans) % 2 == 0 else 1
    for k in range(0, len(spans), step):
        span = slice(spans[k] * count, (spans[k] + step) * count)
        coarse, fine = product(stacked[...], upper, high[:, span], low[:, span])
        total = coarse[:half] + coarse[upper:] + fine[:half]
        for i in range(step):
            at = slice(i * count, (i + 1) * count)
            outs[k + i][:half] = total[:, at]
            if with_sums:
                outs[k + i][half:] = coarse[half : half + 8, at] + fine[half : half + 8, at]


def again_kernel(inverse, half, peers, with_sums, *refs):
    blocks, row_points, col_points = refs[:peers], refs[peers], refs[peers + 1]
    outs = refs[peers + 2 : 2 * peers + 2]
    stacked, rows, cols, high, low = refs[2 * peers + 2 :]
    count = blocks[0].shape[1]
    upper = half + (ONES if with_sums else 0)
    rows[...] = point_features(row_points[...], inverse, True)
    cols[...] = point_features(col_points[...], inverse, False)
    if with_sums:
        stacked[half:upper, :] = jnp.full((ONES, count), 4.0, BF16)
    for k in range(peers):
        a, b = parts_of(blocks[k][...] * 4.0, 2)
        stacked[:half] = a
        stacked[upper:] = b
        for j in range(peers):
            mine = rows[:, k * count : (k + 1) * count]
            evaluate(mine, 0, cols[:, j * count : (j + 1) * count], high, low, 0, 128)
            coarse, fine = product(stacked[...], upper, high[...], low[...])
            total = coarse[:half] + coarse[upper:] + fine[:half]
            outs[j][:half] = total if k == 0 else outs[j][:half] + total
            if with_sums:
                sums = coarse[half : half + 8] + fine[half : half + 8]
                outs[j][half:] = sums if k == 0 else outs[j][half:] + sums


def vmem(count):
    return [pl.BlockSpec(memory_space=pltpu.VMEM)] * count


def params():
    return pltpu.CompilerParams(vmem_limit_bytes=24 << 20)


def cost(rows, cols, half, evaluated):
    return pl.CostEstimate(
        flops=rows * cols * (6 * half + (200 if evaluated else 0)), bytes_accessed=4 * rows * half, transcendentals=0
    )


def per_device(vol_grad, vol_coords, ctrl_coords):
    tgt, src = lax.axis_size("tgt"), lax.axis_size("src")
    chips = src // 2
    peers = tgt
    if chips != tgt or src % 2 or tgt & (tgt - 1):
        raise ValueError("unsupported mesh")
    half = vol_grad.shape[0] // 2
    volume, owned = vol_grad.shape[1], ctrl_coords.shape[1]
    overall = owned * tgt * src
    radius = (3.0 * neighbours / (4.0 * math.pi * overall)) ** (1.0 / 3.0)
    inverse = 1.0 / radius
    core = lax.axis_index("src") % 2
    first_core = core == 0

    sibling = [(i, i ^ 1) for i in range(src)]

    def moved(flips):
        return [
            ((t * chips + c) * 2 + r, ((t ^ flips[r][0]) * chips + (c ^ flips[r][1])) * 2 + r)
            for t in range(tgt)
            for c in range(chips)
            for r in range(2)
        ]

    along_src = [moved(((0, k), (0, k))) for k in range(peers)]
    along_tgt = [moved(((k, 0), (k, 0))) for k in range(peers)]
    gather_pairs = [moved(((0, k), (k, 0))) for k in range(peers)]
    sum_pairs = [moved(((k, 0), (0, k))) for k in range(peers)]

    def exchange(value, pairs):
        return lax.ppermute(value, ("tgt", "src"), pairs)

    def ordered(mine, other, axis):
        return jnp.where(
            first_core, jnp.concatenate([mine, other], axis=axis), jnp.concatenate([other, mine], axis=axis)
        )

    block = jnp.concatenate(
        [
            vol_grad,
            vol_coords,
            jnp.pad(ctrl_coords, ((0, 0), (0, volume - owned))),
            jnp.zeros((COORDS - 6, volume), F32),
        ],
        axis=0,
    )
    ctrl = ordered(ctrl_coords, lax.ppermute(ctrl_coords, "src", sibling), 1)
    blocks = [block] + [exchange(block, along_src[k]) for k in range(1, peers)]
    tgt_ctrl = [ctrl] + [exchange(ctrl, along_tgt[k]) for k in range(1, peers)]

    width, full = 2 * owned, 2 * half
    total_width = peers * width
    core_of = jnp.reshape(core, (1,)).astype(jnp.int32)
    scalar = [pl.BlockSpec(memory_space=pltpu.SMEM)]
    span_step = 2 if peers % 4 == 0 else 1
    pull_scratch = [
        pltpu.VMEM((2 * full, volume), BF16),
        pltpu.VMEM((FEATURES, volume), BF16),
        pltpu.VMEM((volume, span_step * width), BF16),
        pltpu.VMEM((volume, span_step * width), BF16),
    ]

    def pull(which, spans, cols, before, last):
        first = which == 0
        sums = pltpu.VMEM((full, total_width), F32)
        if last:
            shapes = [jax.ShapeDtypeStruct((half, width), F32)] * len(spans)
            shapes.append(jax.ShapeDtypeStruct((half, len(spans) * width), F32))
        else:
            shapes = [pltpu.VMEM((FEATURES, total_width), BF16), sums] if first else [sums]
        if first:
            inputs = [core_of, blocks[which], *tgt_ctrl]
        else:
            inputs = [core_of, blocks[which]]
            inputs += [pltpu.with_memory_space_constraint(value, pltpu.VMEM) for value in (cols, before)]
        return pl.pallas_call(
            functools.partial(pull_kernel, inverse, full, spans, first, last),
            out_shape=shapes,
            in_specs=scalar + vmem(len(inputs) - 1),
            out_specs=vmem(len(shapes)),
            scratch_shapes=pull_scratch,
            input_output_aliases={} if first or last else {3: 0},
            compiler_params=params(),
            cost_estimate=cost(volume, len(spans) * width, full, True),
        )(*inputs)

    near, far = list(range(peers // 2)), list(range(peers // 2, peers))
    cols, sofar = pull(0, near + far, None, None, False)
    for k in range(1, peers - 1):
        (sofar,) = pull(k, near + far, cols, sofar, False)
    sums = [None] * peers
    for spans in (far, near):
        *mine, other = pull(peers - 1, spans, cols, sofar, True)
        other = lax.ppermute(other, "src", sibling)
        for i, k in enumerate(spans):
            sums[k] = mine[i] + other[:, i * width : (i + 1) * width]

    def summed(values):
        total = values[0]
        for k in range(1, peers):
            total = total + exchange(values[k], sum_pairs[k])
        return total

    theirs = jnp.concatenate([b[full + 3 : full + 6, :owned] for b in blocks[1:]], axis=1)
    others = lax.ppermute(theirs, "src", sibling)
    src_points = [ctrl]
    for k in range(peers - 1):
        at = slice(k * owned, (k + 1) * owned)
        src_points.append(ordered(theirs[:, at], others[:, at], 1))
    src_points = jnp.concatenate(src_points, axis=1)
    tgt_points = jnp.concatenate(tgt_ctrl, axis=1)
    row_points = jnp.where(first_core, src_points, tgt_points)
    col_points = jnp.where(first_core, tgt_points, src_points)

    kept = (peers * width) ** 2 * 4 <= KEPT_BYTES
    pullback = sums[0]
    if kept:
        high, low, zero = pl.pallas_call(
            functools.partial(keep_kernel, inverse),
            out_shape=[pltpu.VMEM((peers * width, peers * width), BF16)] * 2 + [jax.ShapeDtypeStruct((8, 128), F32)],
            in_specs=vmem(2),
            out_specs=vmem(3),
            scratch_shapes=[pltpu.VMEM((FEATURES, peers * width), BF16)] * 2,
            compiler_params=params(),
            cost_estimate=cost(peers * width, peers * width, 0, True),
        )(row_points, col_points)
        pullback = pullback + zero[0, 0]
    for k in range(1, peers):
        pullback = pullback + exchange(sums[k], along_tgt[k])

    iterate = pullback
    for sweep in range(STEPS):
        arrived = [iterate] + [exchange(iterate, gather_pairs[k]) for k in range(1, peers)]
        with_sums = sweep == 0
        upper = half + (ONES if with_sums else 0)
        out_rows = half + (8 if with_sums else 0)
        products = [None] * peers
        if kept:
            for spans in (far, near):
                found = pl.pallas_call(
                    functools.partial(step_kernel, half, peers, spans, with_sums),
                    out_shape=[jax.ShapeDtypeStruct((out_rows, width), F32)] * len(spans),
                    in_specs=vmem(peers + 2),
                    out_specs=vmem(len(spans)),
                    scratch_shapes=[pltpu.VMEM((upper + half, peers * width), BF16)],
                    compiler_params=params(),
                    cost_estimate=cost(peers * width, len(spans) * width, half, False),
                )(
                    *arrived,
                    pltpu.with_memory_space_constraint(high, pltpu.VMEM),
                    pltpu.with_memory_space_constraint(low, pltpu.VMEM),
                )
                for k, value in zip(spans, found):
                    products[k] = value
        else:
            products = pl.pallas_call(
                functools.partial(again_kernel, inverse, half, peers, with_sums),
                out_shape=[jax.ShapeDtypeStruct((out_rows, width), F32)] * peers,
                in_specs=vmem(peers + 2),
                out_specs=vmem(peers),
                scratch_shapes=[
                    pltpu.VMEM((upper + half, width), BF16),
                    pltpu.VMEM((FEATURES, peers * width), BF16),
                    pltpu.VMEM((FEATURES, peers * width), BF16),
                    pltpu.VMEM((width, width), BF16),
                    pltpu.VMEM((width, width), BF16),
                ],
                compiler_params=params(),
                cost_estimate=cost(peers * width, peers * width, half, True),
            )(*arrived, row_points, col_points)
        total = summed(products)
        if with_sums:
            scaling = 1.0 / (total[half : half + 1] + ridge_term)
        iterate = iterate + omegas[sweep] * scaling * (pullback - total[:half] - iterate)

    own = jnp.where(first_core, iterate[:, :owned], iterate[:, owned:])
    theirs = jnp.where(first_core, iterate[:, owned:], iterate[:, :owned])
    back = lax.ppermute(theirs, "src", sibling)
    return jnp.where(
        first_core, jnp.concatenate([own, back], axis=0), jnp.concatenate([back, own], axis=0)
    )


def solution(mesh):
    placed = (P(None, ("tgt", "src")), P(None, ("tgt", "src")), P(None, ("tgt", "src")))
    return jax.shard_map(
        per_device, mesh=mesh, in_specs=placed, out_specs=P(None, ("tgt", "src")), check_vma=False
    )
```

```python
import functools
import math

import jax
import jax.numpy as jnp
from jax import lax
from jax.experimental import pallas as pl
from jax.experimental.pallas import tpu as pltpu
from jax.sharding import PartitionSpec as P

STEPS = 2
COORDS = 8
FEATURES = 32
ONES = 16
KEPT_BYTES = 20 << 20

neighbours = 64.0
ridge_term = 1.0
omegas = [1.0 / (0.55 + 0.45 * math.cos(math.pi * (2 * k + 1) / 4.0)) for k in range(2)]

BF16 = jnp.bfloat16
F32 = jnp.float32


def parts_of(value, count):
    terms = []
    for _ in range(count):
        term = value.astype(BF16)
        terms.append(term)
        value = value - term.astype(F32)
    return terms


def point_features(points, inverse, as_rows):
    scaled = (points - 0.5) * inverse
    axes = [scaled[d : d + 1] for d in range(3)]
    norm = parts_of(axes[0] * axes[0] + axes[1] * axes[1] + axes[2] * axes[2], 3)
    one = jnp.ones_like(norm[0])
    found = []
    for axis in axes:
        if as_rows:
            a, b, c = parts_of(-2.0 * axis, 3)
            found += [a, a, b, b, a, c]
        else:
            a, b, c = parts_of(axis, 3)
            found += [a, b, a, b, c, a]
    found += norm + [one] * 3 if as_rows else [one] * 3 + norm
    found += [jnp.zeros_like(one)] * (FEATURES - len(found))
    return jnp.concatenate([f.astype(F32) for f in found], axis=0).astype(BF16)


def quarter_wendland(square):
    square = jnp.minimum(jnp.maximum(square, 1e-12), 1.0)
    distance = square * lax.rsqrt(square)
    falloff = 1.0 - distance
    falloff = falloff * falloff
    return (falloff * falloff) * (distance + 0.25)


def evaluate(rows, row_start, cols, high, low, high_start, sub):
    count, width = rows.shape[1], cols.shape[1]
    for at in range(0, count, sub):
        square = lax.dot_general(
            rows[:, at : at + sub], cols, (((0,), (0,)), ((), ())), preferred_element_type=F32
        )
        value = quarter_wendland(square)
        rounded = value.astype(BF16)
        high[row_start + at : row_start + at + sub, high_start : high_start + width] = rounded
        low[row_start + at : row_start + at + sub, high_start : high_start + width] = (
            value - rounded.astype(F32)
        ).astype(BF16)


def product(stacked, half, high, low):
    coarse = jnp.dot(stacked, high, preferred_element_type=F32)
    fine = jnp.dot(stacked[:half], low, preferred_element_type=F32)
    return coarse, fine


def pull_kernel(inverse, full, width, count, spans, skip, first, last, after_other, *refs):
    refs = list(refs)
    core = refs.pop(0)
    blocks = [refs.pop(0) for _ in range(count)]
    if first == "features":
        sources = [refs.pop(0) for _ in range(after_other)]
        cols, after = refs.pop(0), refs.pop(0)
    else:
        cols = refs.pop(0)
        before = None if first else refs.pop(0)
        del refs[:after_other]
        after = [refs.pop(0) for _ in range(len(spans) + 1)] if last else refs.pop(0)
    stacked, rows, high, low = refs
    half = full // 2
    if first == "features":
        for k, source in enumerate(sources):
            cols[:, k * width : (k + 1) * width] = point_features(source[...], inverse, False)
    step = 2 if len(spans) % 2 == 0 else 1
    sums = [None] * len(spans)
    for n in range(count):
        a, b = parts_of(blocks[n][:full] * 4.0, 2)
        stacked[:full] = a
        stacked[full:] = b
        rows[...] = point_features(blocks[n][full : full + 3], inverse, True)
        for k in range(0, len(spans), step):
            evaluate(rows, 0, cols[:, spans[k] * width : (spans[k] + step) * width], high, low, 0, 128)
            coarse, fine = product(stacked[...], full, high[...], low[...])
            total = coarse[:full] + coarse[full:] + fine
            at = slice(k * width, (k + step) * width)
            if n:
                total = sums[k] + total
            elif not first:
                total = before[:, skip + at.start : skip + at.stop] + total
            sums[k] = total
            if n < count - 1:
                continue
            if not last:
                after[:, at] = total
                continue
            mine = jnp.where(core[0] == 0, total[:half], total[half:])
            for i in range(step):
                after[k + i][...] = mine[:, i * width : (i + 1) * width]
            after[-1][:, at] = jnp.where(core[0] == 0, total[half:], total[:half])


def keep_kernel(inverse, start, row_points, col_points, high, low, zero, rows, cols):
    zero[...] = jnp.zeros_like(zero)
    rows[...] = point_features(row_points[:, start : start + rows.shape[1]], inverse, True)
    cols[...] = point_features(col_points[...], inverse, False)
    count, width = rows.shape[1], math.gcd(cols.shape[1], 1024)
    sub = math.gcd(count, 256)

    def tile(which, carry):
        at = pl.ds(pl.multiple_of(which * width, width), width)
        wide = cols[:, at]
        for row in range(0, count, sub):
            square = lax.dot_general(
                rows[:, row : row + sub], wide, (((0,), (0,)), ((), ())), preferred_element_type=F32
            )
            value = quarter_wendland(square)
            rounded = value.astype(BF16)
            high[row : row + sub, at] = rounded
            low[row : row + sub, at] = (value - rounded.astype(F32)).astype(BF16)
        return carry

    lax.fori_loop(0, cols.shape[1] // width, tile, 0)


def step_kernel(half, start, count, spans, with_sums, first, last, *refs):
    refs = list(refs)
    blocks = [refs.pop(0) for _ in range(count)]
    high, low = refs.pop(0), refs.pop(0)
    before = None if first else refs.pop(0)
    del refs[:1]
    stacked, outs = refs[-1], refs[:-1]
    size = blocks[0].shape[1]
    upper = half + (ONES if with_sums else 0)
    for k in range(count):
        a, b = parts_of(blocks[k][...] * 4.0, 2)
        stacked[:half, k * size : (k + 1) * size] = a
        stacked[upper:, k * size : (k + 1) * size] = b
    if with_sums:
        stacked[half:upper, :] = jnp.full((ONES, stacked.shape[1]), 4.0, BF16)
    step = 2 if len(spans) % 2 == 0 else 1
    along = slice(start * size, (start + count) * size)
    for k in range(0, len(spans), step):
        span = slice(spans[k] * size, (spans[k] + step) * size)
        coarse, fine = product(stacked[...], upper, high[along, span], low[along, span])
        total = coarse[:half] + coarse[upper:] + fine[:half]
        sums = coarse[half : half + 8] + fine[half : half + 8] if with_sums else None
        if not first:
            total = before[:half, span] + total
            sums = before[half:, span] + sums if with_sums else None
        if not last:
            outs[0][:half, span] = total
            if with_sums:
                outs[0][half:, span] = sums
            continue
        for i in range(step):
            at = slice(i * size, (i + 1) * size)
            outs[k + i][:half] = total[:, at]
            if with_sums:
                outs[k + i][half:] = sums[:, at]


def again_kernel(inverse, half, peers, with_sums, *refs):
    blocks, row_points, col_points = refs[:peers], refs[peers], refs[peers + 1]
    outs = refs[peers + 2 : 2 * peers + 2]
    stacked, rows, cols, high, low = refs[2 * peers + 2 :]
    count = blocks[0].shape[1]
    upper = half + (ONES if with_sums else 0)
    rows[...] = point_features(row_points[...], inverse, True)
    cols[...] = point_features(col_points[...], inverse, False)
    if with_sums:
        stacked[half:upper, :] = jnp.full((ONES, count), 4.0, BF16)
    for k in range(peers):
        a, b = parts_of(blocks[k][...] * 4.0, 2)
        stacked[:half] = a
        stacked[upper:] = b
        for j in range(peers):
            mine = rows[:, k * count : (k + 1) * count]
            evaluate(mine, 0, cols[:, j * count : (j + 1) * count], high, low, 0, 128)
            coarse, fine = product(stacked[...], upper, high[...], low[...])
            total = coarse[:half] + coarse[upper:] + fine[:half]
            outs[j][:half] = total if k == 0 else outs[j][:half] + total
            if with_sums:
                sums = coarse[half : half + 8] + fine[half : half + 8]
                outs[j][half:] = sums if k == 0 else outs[j][half:] + sums


def vmem(count):
    return [pl.BlockSpec(memory_space=pltpu.VMEM)] * count


def params():
    return pltpu.CompilerParams(vmem_limit_bytes=24 << 20)


def cost(rows, half, weight=1):
    return pl.CostEstimate(flops=rows * half * weight, bytes_accessed=half, transcendentals=0)


def per_device(vol_grad, vol_coords, ctrl_coords):
    tgt, src = lax.axis_size("tgt"), lax.axis_size("src")
    chips = src // 2
    peers = tgt
    if chips != tgt or src % 2 or tgt & (tgt - 1):
        raise ValueError("unsupported mesh")
    half = vol_grad.shape[0] // 2
    volume, owned = vol_grad.shape[1], ctrl_coords.shape[1]
    overall = owned * tgt * src
    radius = (3.0 * neighbours / (4.0 * math.pi * overall)) ** (1.0 / 3.0)
    inverse = 1.0 / radius
    core = lax.axis_index("src") % 2
    first_core = core == 0

    sibling = [(i, i ^ 1) for i in range(src)]

    def moved(flips):
        return [
            ((t * chips + c) * 2 + r, ((t ^ flips[r][0]) * chips + (c ^ flips[r][1])) * 2 + r)
            for t in range(tgt)
            for c in range(chips)
            for r in range(2)
        ]

    along_src = [moved(((0, k), (0, k))) for k in range(peers)]
    along_tgt = [moved(((k, 0), (k, 0))) for k in range(peers)]
    gather_pairs = [moved(((0, k), (k, 0))) for k in range(peers)]
    sum_pairs = [moved(((k, 0), (0, k))) for k in range(peers)]

    def exchange(value, pairs):
        return lax.ppermute(value, ("tgt", "src"), pairs)

    def ordered(mine, other, axis):
        return jnp.where(
            first_core, jnp.concatenate([mine, other], axis=axis), jnp.concatenate([other, mine], axis=axis)
        )

    block = jnp.concatenate(
        [
            vol_grad,
            vol_coords,
            jnp.pad(ctrl_coords, ((0, 0), (0, volume - owned))),
            jnp.zeros((COORDS - 6, volume), F32),
        ],
        axis=0,
    )
    got = lax.ppermute(ctrl_coords, "src", sibling)
    block, got = lax.optimization_barrier((block, got))
    ctrl = ordered(ctrl_coords, got, 1)
    blocks = [block] + [exchange(block, along_src[k]) for k in range(1, peers)]
    tgt_ctrl = [ctrl] + [exchange(ctrl, along_tgt[k]) for k in range(1, peers)]

    width, full = 2 * owned, 2 * half
    total_width = peers * width
    core_of = jnp.reshape(core, (1,)).astype(jnp.int32)
    scalar = [pl.BlockSpec(memory_space=pltpu.SMEM)]
    anywhere = [pl.BlockSpec(memory_space=pl.ANY)]
    def pull(which, spans, cols, before, last, skip=0, other=(), weight=1):
        first = before is None
        step = 2 if len(spans) % 2 == 0 else 1
        if last:
            shapes = [jax.ShapeDtypeStruct((half, width), F32)] * len(spans)
            shapes.append(jax.ShapeDtypeStruct((half, len(spans) * width), F32))
        else:
            shapes = [pltpu.VMEM((full, len(spans) * width), F32)]
        inputs = [core_of, *[blocks[k] for k in which]]
        if cols is None:
            first = "features"
            shapes = [pltpu.VMEM((FEATURES, total_width), BF16)] + shapes
            inputs += tgt_ctrl
        else:
            inputs.append(pltpu.with_memory_space_constraint(cols, pltpu.VMEM))
        if not first:
            inputs.append(pltpu.with_memory_space_constraint(before, pltpu.VMEM))
        in_specs = scalar + vmem(len(inputs) - 1) + anywhere * len(other)
        inputs += other
        extra = len(tgt_ctrl) if cols is None else len(other)
        return pl.pallas_call(
            functools.partial(
                pull_kernel, inverse, full, width, len(which), spans, skip, first, last, extra
            ),
            out_shape=shapes,
            in_specs=in_specs,
            out_specs=vmem(len(shapes)),
            scratch_shapes=[
                pltpu.VMEM((2 * full, volume), BF16),
                pltpu.VMEM((FEATURES, volume), BF16),
                pltpu.VMEM((volume, step * width), BF16),
                pltpu.VMEM((volume, step * width), BF16),
            ],
            compiler_params=params(),
            cost_estimate=cost(len(which) * volume, full, weight),
        )(*inputs)

    near, far = list(range(peers // 2)), list(range(peers // 2, peers))
    cols, far_sofar = pull([0], far, None, None, False)
    (near_sofar,) = pull([0], near, cols, None, False)
    sums = [None] * peers
    arriving = list(range(1, peers))

    theirs = jnp.concatenate([b[full + 3 : full + 6, :owned] for b in blocks[1:]], axis=1)
    others = lax.ppermute(theirs, "src", sibling)
    src_points = [ctrl]
    for k in range(peers - 1):
        at = slice(k * owned, (k + 1) * owned)
        src_points.append(ordered(theirs[:, at], others[:, at], 1))
    src_points = jnp.concatenate(src_points, axis=1)
    tgt_points = jnp.concatenate(tgt_ctrl, axis=1)
    row_points = jnp.where(first_core, src_points, tgt_points)
    col_points = jnp.where(first_core, tgt_points, src_points)

    def added(spans, mine, other, pieces=1):
        rows = half // pieces
        other = [lax.ppermute(other[i * rows : (i + 1) * rows], "src", sibling) for i in range(pieces)]
        other = jnp.concatenate(other, axis=0)
        for i, k in enumerate(spans):
            sums[k] = mine[i] + other[:, i * width : (i + 1) * width]

    *mine, other = pull(arriving, far, cols, far_sofar, True, weight=8 * width)
    added(far, mine, other)
    if near[1:]:
        *mine, other = pull(arriving, near[1:], cols, near_sofar, True, width, [other], 4 * width)
        added(near[1:], mine, other)
    *mine, other = pull(arriving, near[:1], cols, near_sofar, True, 0, [sums[k] for k in range(1, peers)] + [row_points, col_points])
    added(near[:1], mine, other, 2)

    def summed(values):
        order = [peers // 2] + [k for k in range(1, peers) if k != peers // 2]
        got = {k: exchange(values[k], sum_pairs[k]) for k in order}
        total = values[0]
        for k in order:
            total = total + got[k]
        return total

    kept = (peers * width) ** 2 * 4 <= KEPT_BYTES
    pullback = sums[0]
    def keep(start, count):
        return pl.pallas_call(
            functools.partial(keep_kernel, inverse, start * width),
            out_shape=[pltpu.VMEM((count * width, total_width), BF16)] * 2
            + [jax.ShapeDtypeStruct((1, width), F32)],
            in_specs=vmem(2),
            out_specs=vmem(3),
            scratch_shapes=[pltpu.VMEM((FEATURES, count * width), BF16), pltpu.VMEM((FEATURES, total_width), BF16)],
            compiler_params=params(),
            cost_estimate=cost(total_width, half),
        )(row_points, col_points)

    if kept:
        *early, zero = keep(0, peers - 1)
        *final, after_final = keep(peers - 1, 1)
        pullback = pullback + zero

    def step(these, part, start, spans, before, with_sums, last, other):
        out_rows = half + (8 if with_sums else 0)
        if last:
            shapes = [jax.ShapeDtypeStruct((out_rows, width), F32)] * len(spans)
        else:
            shapes = [pltpu.VMEM((out_rows, total_width), F32)]
        inputs = these + [pltpu.with_memory_space_constraint(value, pltpu.VMEM) for value in part]
        if before is not None:
            inputs.append(pltpu.with_memory_space_constraint(before, pltpu.VMEM))
        upper = half + (ONES if with_sums else 0)
        return pl.pallas_call(
            functools.partial(
                step_kernel, half, start, len(these), spans, with_sums, before is None, last
            ),
            out_shape=shapes,
            in_specs=vmem(len(inputs)) + anywhere,
            out_specs=vmem(len(shapes)),
            scratch_shapes=[pltpu.VMEM((upper + half, len(these) * width), BF16)],
            compiler_params=params(),
            cost_estimate=cost(total_width, half),
        )(*inputs, other)

    for k in range(1, peers):
        pullback = pullback + exchange(sums[k], along_tgt[k])

    iterate = pullback
    for sweep in range(STEPS):
        arrived = [iterate] + [exchange(iterate, gather_pairs[k]) for k in range(1, peers)]
        with_sums = sweep == 0
        if kept:
            spans = near + far
            (sofar,) = step(arrived[:1], early, 0, spans, None, with_sums, False, after_final)
            if peers > 2:
                (sofar,) = step(arrived[1:-1], early, 1, spans, sofar, with_sums, False, after_final)
            far_ones = step(arrived[-1:], final, 0, far, sofar, with_sums, True, after_final)
            near_ones = step(arrived[-1:], final, 0, near, sofar, with_sums, True, far_ones[0])
            products = [*near_ones, *far_ones]
        else:
            upper = half + (ONES if with_sums else 0)
            out_rows = half + (8 if with_sums else 0)
            products = pl.pallas_call(
                functools.partial(again_kernel, inverse, half, peers, with_sums),
                out_shape=[jax.ShapeDtypeStruct((out_rows, width), F32)] * peers,
                in_specs=vmem(peers + 2),
                out_specs=vmem(peers),
                scratch_shapes=[
                    pltpu.VMEM((upper + half, width), BF16),
                    pltpu.VMEM((FEATURES, peers * width), BF16),
                    pltpu.VMEM((FEATURES, peers * width), BF16),
                    pltpu.VMEM((width, width), BF16),
                    pltpu.VMEM((width, width), BF16),
                ],
                compiler_params=params(),
                cost_estimate=cost(total_width, half),
            )(*arrived, row_points, col_points)
        total = summed(products)
        if with_sums:
            scaling = 1.0 / (total[half : half + 1] + ridge_term)
        iterate = iterate + omegas[sweep] * scaling * (pullback - total[:half] - iterate)

    own = jnp.where(first_core, iterate[:, :owned], iterate[:, owned:])
    theirs = jnp.where(first_core, iterate[:, owned:], iterate[:, :owned])
    back = lax.ppermute(theirs, "src", sibling)
    return jnp.where(
        first_core, jnp.concatenate([own, back], axis=0), jnp.concatenate([back, own], axis=0)
    )


def solution(mesh):
    placed = (P(None, ("tgt", "src")), P(None, ("tgt", "src")), P(None, ("tgt", "src")))
    return jax.shard_map(
        per_device, mesh=mesh, in_specs=placed, out_specs=P(None, ("tgt", "src")), check_vma=False
    )
```

```python
import functools
import math

import jax
import jax.numpy as jnp
from jax import lax
from jax.experimental import pallas as pl
from jax.experimental.pallas import tpu as pltpu
from jax.sharding import PartitionSpec as P

STEPS = 2
COORDS = 8
FEATURES = 32
ONES = 16
KEPT_BYTES = 20 << 20

neighbours = 64.0
ridge_term = 1.0
omegas = [1.0 / (0.55 + 0.45 * math.cos(math.pi * (2 * k + 1) / 4.0)) for k in range(2)]

BF16 = jnp.bfloat16
F32 = jnp.float32


def parts_of(value, count):
    terms = []
    for _ in range(count):
        term = value.astype(BF16)
        terms.append(term)
        value = value - term.astype(F32)
    return terms


def point_features(points, inverse, as_rows):
    scaled = (points - 0.5) * inverse
    axes = [scaled[d : d + 1] for d in range(3)]
    norm = parts_of(axes[0] * axes[0] + axes[1] * axes[1] + axes[2] * axes[2], 3)
    one = jnp.ones_like(norm[0])
    found = []
    for axis in axes:
        if as_rows:
            a, b, c = parts_of(-2.0 * axis, 3)
            found += [a, a, b, b, a, c]
        else:
            a, b, c = parts_of(axis, 3)
            found += [a, b, a, b, c, a]
    found += norm + [one] * 3 if as_rows else [one] * 3 + norm
    found += [jnp.zeros_like(one)] * (FEATURES - len(found))
    return jnp.concatenate([f.astype(F32) for f in found], axis=0).astype(BF16)


def quarter_wendland(square):
    square = jnp.minimum(jnp.maximum(square, 1e-12), 1.0)
    distance = square * lax.rsqrt(square)
    falloff = 1.0 - distance
    falloff = falloff * falloff
    return (falloff * falloff) * (distance + 0.25)


def evaluate(rows, row_start, cols, high, low, high_start, sub):
    count, width = rows.shape[1], cols.shape[1]
    for at in range(0, count, sub):
        square = lax.dot_general(
            rows[:, at : at + sub], cols, (((0,), (0,)), ((), ())), preferred_element_type=F32
        )
        value = quarter_wendland(square)
        rounded = value.astype(BF16)
        high[row_start + at : row_start + at + sub, high_start : high_start + width] = rounded
        low[row_start + at : row_start + at + sub, high_start : high_start + width] = (
            value - rounded.astype(F32)
        ).astype(BF16)


def product(stacked, half, high, low):
    coarse = jnp.dot(stacked, high, preferred_element_type=F32)
    fine = jnp.dot(stacked[:half], low, preferred_element_type=F32)
    return coarse, fine


def pull_kernel(inverse, full, width, count, spans, skip, first, last, after_other, *refs):
    refs = list(refs)
    core = refs.pop(0)
    blocks = [refs.pop(0) for _ in range(count)]
    if first == "features":
        sources = [refs.pop(0) for _ in range(after_other)]
        cols, after = refs.pop(0), refs.pop(0)
    else:
        cols = refs.pop(0)
        before = None if first else refs.pop(0)
        del refs[:after_other]
        after = [refs.pop(0) for _ in range(len(spans) + 1)] if last else refs.pop(0)
    stacked, rows, high, low = refs
    half = full // 2
    if first == "features":
        for k, source in enumerate(sources):
            cols[:, k * width : (k + 1) * width] = point_features(source[...], inverse, False)
    step = 2 if len(spans) % 2 == 0 else 1
    sums = [None] * len(spans)
    for n in range(count):
        a, b = parts_of(blocks[n][:full] * 4.0, 2)
        stacked[:full] = a
        stacked[full:] = b
        rows[...] = point_features(blocks[n][full : full + 3], inverse, True)
        for k in range(0, len(spans), step):
            evaluate(rows, 0, cols[:, spans[k] * width : (spans[k] + step) * width], high, low, 0, 128)
            coarse, fine = product(stacked[...], full, high[...], low[...])
            total = coarse[:full] + coarse[full:] + fine
            at = slice(k * width, (k + step) * width)
            if n:
                total = sums[k] + total
            elif not first:
                total = before[:, skip + at.start : skip + at.stop] + total
            sums[k] = total
            if n < count - 1:
                continue
            if not last:
                after[:, at] = total
                continue
            mine = jnp.where(core[0] == 0, total[:half], total[half:])
            for i in range(step):
                after[k + i][...] = mine[:, i * width : (i + 1) * width]
            after[-1][:, at] = jnp.where(core[0] == 0, total[half:], total[:half])


def keep_kernel(inverse, start, row_points, col_points, high, low, zero, rows, cols):
    zero[...] = jnp.zeros_like(zero)
    rows[...] = point_features(row_points[:, start : start + rows.shape[1]], inverse, True)
    cols[...] = point_features(col_points[...], inverse, False)
    count, width = rows.shape[1], math.gcd(cols.shape[1], 1024)
    sub = math.gcd(count, 256)

    def tile(which, carry):
        at = pl.ds(pl.multiple_of(which * width, width), width)
        wide = cols[:, at]
        for row in range(0, count, sub):
            square = lax.dot_general(
                rows[:, row : row + sub], wide, (((0,), (0,)), ((), ())), preferred_element_type=F32
            )
            value = quarter_wendland(square)
            rounded = value.astype(BF16)
            high[row : row + sub, at] = rounded
            low[row : row + sub, at] = (value - rounded.astype(F32)).astype(BF16)
        return carry

    lax.fori_loop(0, cols.shape[1] // width, tile, 0)


def step_kernel(half, start, count, spans, with_sums, first, last, *refs):
    refs = list(refs)
    blocks = [refs.pop(0) for _ in range(count)]
    high, low = refs.pop(0), refs.pop(0)
    before = None if first else refs.pop(0)
    del refs[:1]
    stacked, outs = refs[-1], refs[:-1]
    size = blocks[0].shape[1]
    upper = half + (ONES if with_sums else 0)
    for k in range(count):
        a, b = parts_of(blocks[k][...] * 4.0, 2)
        stacked[:half, k * size : (k + 1) * size] = a
        stacked[upper:, k * size : (k + 1) * size] = b
    if with_sums:
        stacked[half:upper, :] = jnp.full((ONES, stacked.shape[1]), 4.0, BF16)
    step = 2 if len(spans) % 2 == 0 else 1
    along = slice(start * size, (start + count) * size)
    for k in range(0, len(spans), step):
        span = slice(spans[k] * size, (spans[k] + step) * size)
        coarse, fine = product(stacked[...], upper, high[along, span], low[along, span])
        total = coarse[:half] + coarse[upper:] + fine[:half]
        sums = coarse[half : half + 8] + fine[half : half + 8] if with_sums else None
        if not first:
            total = before[:half, span] + total
            sums = before[half:, span] + sums if with_sums else None
        if not last:
            outs[0][:half, span] = total
            if with_sums:
                outs[0][half:, span] = sums
            continue
        for i in range(step):
            at = slice(i * size, (i + 1) * size)
            outs[k + i][:half] = total[:, at]
            if with_sums:
                outs[k + i][half:] = sums[:, at]


def again_kernel(inverse, half, peers, with_sums, *refs):
    blocks, row_points, col_points = refs[:peers], refs[peers], refs[peers + 1]
    outs = refs[peers + 2 : 2 * peers + 2]
    stacked, rows, cols, high, low = refs[2 * peers + 2 :]
    count = blocks[0].shape[1]
    upper = half + (ONES if with_sums else 0)
    rows[...] = point_features(row_points[...], inverse, True)
    cols[...] = point_features(col_points[...], inverse, False)
    if with_sums:
        stacked[half:upper, :] = jnp.full((ONES, count), 4.0, BF16)
    for k in range(peers):
        a, b = parts_of(blocks[k][...] * 4.0, 2)
        stacked[:half] = a
        stacked[upper:] = b
        for j in range(peers):
            mine = rows[:, k * count : (k + 1) * count]
            evaluate(mine, 0, cols[:, j * count : (j + 1) * count], high, low, 0, 128)
            coarse, fine = product(stacked[...], upper, high[...], low[...])
            total = coarse[:half] + coarse[upper:] + fine[:half]
            outs[j][:half] = total if k == 0 else outs[j][:half] + total
            if with_sums:
                sums = coarse[half : half + 8] + fine[half : half + 8]
                outs[j][half:] = sums if k == 0 else outs[j][half:] + sums


def vmem(count):
    return [pl.BlockSpec(memory_space=pltpu.VMEM)] * count


def params():
    return pltpu.CompilerParams(vmem_limit_bytes=24 << 20)


def cost(rows, half, weight=1):
    return pl.CostEstimate(flops=rows * half * weight, bytes_accessed=half, transcendentals=0)


def per_device(vol_grad, vol_coords, ctrl_coords):
    tgt, src = lax.axis_size("tgt"), lax.axis_size("src")
    chips = src // 2
    peers = tgt
    if chips != tgt or src % 2 or tgt & (tgt - 1):
        raise ValueError("unsupported mesh")
    half = vol_grad.shape[0] // 2
    volume, owned = vol_grad.shape[1], ctrl_coords.shape[1]
    overall = owned * tgt * src
    radius = (3.0 * neighbours / (4.0 * math.pi * overall)) ** (1.0 / 3.0)
    inverse = 1.0 / radius
    core = lax.axis_index("src") % 2
    first_core = core == 0

    sibling = [(i, i ^ 1) for i in range(src)]

    def moved(flips):
        return [
            ((t * chips + c) * 2 + r, ((t ^ flips[r][0]) * chips + (c ^ flips[r][1])) * 2 + r)
            for t in range(tgt)
            for c in range(chips)
            for r in range(2)
        ]

    along_src = [moved(((0, k), (0, k))) for k in range(peers)]
    along_tgt = [moved(((k, 0), (k, 0))) for k in range(peers)]
    gather_pairs = [moved(((0, k), (k, 0))) for k in range(peers)]
    sum_pairs = [moved(((k, 0), (0, k))) for k in range(peers)]

    def exchange(value, pairs):
        return lax.ppermute(value, ("tgt", "src"), pairs)

    def ordered(mine, other, axis):
        return jnp.where(
            first_core, jnp.concatenate([mine, other], axis=axis), jnp.concatenate([other, mine], axis=axis)
        )

    block = jnp.concatenate(
        [
            vol_grad,
            vol_coords,
            jnp.pad(ctrl_coords, ((0, 0), (0, volume - owned))),
            jnp.zeros((COORDS - 6, volume), F32),
        ],
        axis=0,
    )
    got = lax.ppermute(ctrl_coords, "src", sibling)
    block, got = lax.optimization_barrier((block, got))
    ctrl = ordered(ctrl_coords, got, 1)
    blocks = [block] + [exchange(block, along_src[k]) for k in range(1, peers)]
    tgt_ctrl = [ctrl] + [exchange(ctrl, along_tgt[k]) for k in range(1, peers)]

    width, full = 2 * owned, 2 * half
    total_width = peers * width
    core_of = jnp.reshape(core, (1,)).astype(jnp.int32)
    scalar = [pl.BlockSpec(memory_space=pltpu.SMEM)]
    anywhere = [pl.BlockSpec(memory_space=pl.ANY)]

    def pull(which, spans, cols, before, last, skip=0, other=(), weight=1):
        first = before is None
        step = 2 if len(spans) % 2 == 0 else 1
        if last:
            shapes = [jax.ShapeDtypeStruct((half, width), F32)] * len(spans)
            shapes.append(jax.ShapeDtypeStruct((half, len(spans) * width), F32))
        else:
            shapes = [pltpu.VMEM((full, len(spans) * width), F32)]
        inputs = [core_of, *[blocks[k] for k in which]]
        if cols is None:
            first = "features"
            shapes = [pltpu.VMEM((FEATURES, len(spans) * width), BF16)] + shapes
            inputs += [tgt_ctrl[k] for k in spans]
        else:
            inputs.append(pltpu.with_memory_space_constraint(cols, pltpu.VMEM))
        if not first:
            inputs.append(pltpu.with_memory_space_constraint(before, pltpu.VMEM))
        in_specs = scalar + vmem(len(inputs) - 1) + anywhere * len(other)
        inputs += other
        extra = len(spans) if cols is None else len(other)
        return pl.pallas_call(
            functools.partial(
                pull_kernel, inverse, full, width, len(which), [within[k] for k in spans], skip, first, last, extra
            ),
            out_shape=shapes,
            in_specs=in_specs,
            out_specs=vmem(len(shapes)),
            scratch_shapes=[
                pltpu.VMEM((2 * full, volume), BF16),
                pltpu.VMEM((FEATURES, volume), BF16),
                pltpu.VMEM((volume, step * width), BF16),
                pltpu.VMEM((volume, step * width), BF16),
            ],
            compiler_params=params(),
            cost_estimate=cost(len(which) * volume, full, weight),
        )(*inputs)

    near, far = list(range(peers // 2)), list(range(peers // 2, peers))
    within = {k: k - half_of[0] for half_of in (near, far) for k in half_of}
    near_cols, near_sofar = pull([0], near, None, None, False)
    far_cols, far_sofar = pull([0], far, None, None, False)
    sums = [None] * peers
    arriving = list(range(1, peers))

    def swapped(other, pieces=1):
        rows = half // pieces
        return [lax.ppermute(other[i * rows : (i + 1) * rows], "src", sibling) for i in range(pieces)]

    def added(spans, mine, other):
        other = jnp.concatenate(other, axis=0)
        for i, k in enumerate(spans):
            sums[k] = mine[i] + other[:, i * width : (i + 1) * width]

    if peers > 2:
        (far_sofar,) = pull(arriving[:1], far, far_cols, far_sofar, False, weight=8 * width)
    *mine, other = pull(arriving[1:] or arriving, far, far_cols, far_sofar, True, weight=8 * width)
    late, _ = lax.optimization_barrier((blocks[1:], other))
    theirs = jnp.concatenate([b[full + 3 : full + 6, :owned] for b in late], axis=1)
    others = lax.ppermute(theirs, "src", sibling)
    src_points = [ctrl]
    for k in range(peers - 1):
        at = slice(k * owned, (k + 1) * owned)
        src_points.append(ordered(theirs[:, at], others[:, at], 1))
    src_points = jnp.concatenate(src_points, axis=1)
    tgt_points = jnp.concatenate(tgt_ctrl, axis=1)
    row_points = jnp.where(first_core, src_points, tgt_points)
    col_points = jnp.where(first_core, tgt_points, src_points)
    given = swapped(other)
    if near[1:]:
        *near_mine, other = pull(arriving, near[1:], near_cols, near_sofar, True, width, [other], 4 * width)
        near_given = swapped(other)
    added(far, mine, given)
    *mine, other = pull(
        arriving, near[:1], near_cols, near_sofar, True, 0, [sums[k] for k in far]
    )
    if near[1:]:
        near_given, mine, other = lax.optimization_barrier((near_given, mine, other))
        added(near[1:], near_mine, near_given)
    added(near[:1], mine, swapped(other, 2))

    def summed(values):
        order = [peers // 2] + [k for k in range(1, peers) if k != peers // 2]
        got = {k: exchange(values[k], sum_pairs[k]) for k in order}
        total = values[0]
        for k in order:
            total = total + got[k]
        return total

    kept = (peers * width) ** 2 * 4 <= KEPT_BYTES
    pullback = sums[0]

    def keep(start, count):
        return pl.pallas_call(
            functools.partial(keep_kernel, inverse, start * width),
            out_shape=[pltpu.VMEM((count * width, total_width), BF16)] * 2
            + [jax.ShapeDtypeStruct((1, width), F32)],
            in_specs=vmem(2),
            out_specs=vmem(3),
            scratch_shapes=[pltpu.VMEM((FEATURES, count * width), BF16), pltpu.VMEM((FEATURES, total_width), BF16)],
            compiler_params=params(),
            cost_estimate=cost(total_width, half),
        )(row_points, col_points)

    if kept:
        *early, zero = keep(0, peers - 1)
        *final, after_final = keep(peers - 1, 1)
        pullback = pullback + zero

    def step(these, part, start, spans, before, with_sums, last, other):
        out_rows = half + (8 if with_sums else 0)
        if last:
            shapes = [jax.ShapeDtypeStruct((out_rows, width), F32)] * len(spans)
        else:
            shapes = [pltpu.VMEM((out_rows, total_width), F32)]
        inputs = these + [pltpu.with_memory_space_constraint(value, pltpu.VMEM) for value in part]
        if before is not None:
            inputs.append(pltpu.with_memory_space_constraint(before, pltpu.VMEM))
        upper = half + (ONES if with_sums else 0)
        return pl.pallas_call(
            functools.partial(
                step_kernel, half, start, len(these), spans, with_sums, before is None, last
            ),
            out_shape=shapes,
            in_specs=vmem(len(inputs)) + anywhere,
            out_specs=vmem(len(shapes)),
            scratch_shapes=[pltpu.VMEM((upper + half, len(these) * width), BF16)],
            compiler_params=params(),
            cost_estimate=cost(total_width, half),
        )(*inputs, other)

    got = {k: exchange(sums[k], along_tgt[k]) for k in far + near[1:]}
    for value in got.values():
        pullback = pullback + value

    iterate = pullback
    for sweep in range(STEPS):
        arrived = [iterate] + [exchange(iterate, gather_pairs[k]) for k in range(1, peers)]
        with_sums = sweep == 0
        if kept:
            spans = near + far
            (sofar,) = step(arrived[:1], early, 0, spans, None, with_sums, False, after_final)
            if peers > 2:
                (sofar,) = step(arrived[1:-1], early, 1, spans, sofar, with_sums, False, after_final)
            far_ones = step(arrived[-1:], final, 0, far, sofar, with_sums, True, after_final)
            near_ones = step(arrived[-1:], final, 0, near, sofar, with_sums, True, far_ones[0])
            products = [*near_ones, *far_ones]
        else:
            upper = half + (ONES if with_sums else 0)
            out_rows = half + (8 if with_sums else 0)
            products = pl.pallas_call(
                functools.partial(again_kernel, inverse, half, peers, with_sums),
                out_shape=[jax.ShapeDtypeStruct((out_rows, width), F32)] * peers,
                in_specs=vmem(peers + 2),
                out_specs=vmem(peers),
                scratch_shapes=[
                    pltpu.VMEM((upper + half, width), BF16),
                    pltpu.VMEM((FEATURES, peers * width), BF16),
                    pltpu.VMEM((FEATURES, peers * width), BF16),
                    pltpu.VMEM((width, width), BF16),
                    pltpu.VMEM((width, width), BF16),
                ],
                compiler_params=params(),
                cost_estimate=cost(total_width, half),
            )(*arrived, row_points, col_points)
        total = summed(products)
        if with_sums:
            scaling = 1.0 / (total[half : half + 1] + ridge_term)
        iterate = iterate + omegas[sweep] * scaling * (pullback - total[:half] - iterate)

    own = jnp.where(first_core, iterate[:, :owned], iterate[:, owned:])
    theirs = jnp.where(first_core, iterate[:, owned:], iterate[:, :owned])
    back = lax.ppermute(theirs, "src", sibling)
    return jnp.where(
        first_core, jnp.concatenate([own, back], axis=0), jnp.concatenate([back, own], axis=0)
    )


def solution(mesh):
    placed = (P(None, ("tgt", "src")), P(None, ("tgt", "src")), P(None, ("tgt", "src")))
    return jax.shard_map(
        per_device, mesh=mesh, in_specs=placed, out_specs=P(None, ("tgt", "src")), check_vma=False
    )
```

```python
import functools
import math

import jax
import jax.numpy as jnp
from jax import lax
from jax.experimental import pallas as pl
from jax.experimental.pallas import tpu as pltpu
from jax.sharding import PartitionSpec as P

STEPS = 2
COORDS = 8
FEATURES = 32
ONES = 16
KEPT_BYTES = 20 << 20

neighbours = 64.0
ridge_term = 1.0
omegas = [1.0 / (0.55 + 0.45 * math.cos(math.pi * (2 * k + 1) / 4.0)) for k in range(2)]

BF16 = jnp.bfloat16
F32 = jnp.float32


def parts_of(value, count):
    terms = []
    for _ in range(count):
        term = value.astype(BF16)
        terms.append(term)
        value = value - term.astype(F32)
    return terms


def point_features(points, inverse, as_rows):
    scaled = (points - 0.5) * inverse
    axes = [scaled[d : d + 1] for d in range(3)]
    norm = parts_of(axes[0] * axes[0] + axes[1] * axes[1] + axes[2] * axes[2], 3)
    one = jnp.ones_like(norm[0])
    found = []
    for axis in axes:
        if as_rows:
            a, b, c = parts_of(-2.0 * axis, 3)
            found += [a, a, b, b, a, c]
        else:
            a, b, c = parts_of(axis, 3)
            found += [a, b, a, b, c, a]
    found += norm + [one] * 3 if as_rows else [one] * 3 + norm
    found += [jnp.zeros_like(one)] * (FEATURES - len(found))
    return jnp.concatenate([f.astype(F32) for f in found], axis=0).astype(BF16)


def quarter_wendland(square):
    square = jnp.minimum(jnp.maximum(square, 1e-12), 1.0)
    distance = square * lax.rsqrt(square)
    falloff = 1.0 - distance
    falloff = falloff * falloff
    return (falloff * falloff) * (distance + 0.25)


def evaluate(rows, row_start, cols, high, low, high_start, sub):
    count, width = rows.shape[1], cols.shape[1]
    for at in range(0, count, sub):
        square = lax.dot_general(
            rows[:, at : at + sub], cols, (((0,), (0,)), ((), ())), preferred_element_type=F32
        )
        value = quarter_wendland(square)
        rounded = value.astype(BF16)
        high[row_start + at : row_start + at + sub, high_start : high_start + width] = rounded
        low[row_start + at : row_start + at + sub, high_start : high_start + width] = (
            value - rounded.astype(F32)
        ).astype(BF16)


def product(stacked, half, high, low):
    coarse = jnp.dot(stacked, high, preferred_element_type=F32)
    fine = jnp.dot(stacked[:half], low, preferred_element_type=F32)
    return coarse, fine


def pull_kernel(inverse, full, width, count, spans, skip, first, last, after_other, *refs):
    refs = list(refs)
    core = refs.pop(0)
    blocks = [refs.pop(0) for _ in range(count)]
    if first == "features":
        sources = [refs.pop(0) for _ in range(after_other)]
        cols, after = refs.pop(0), refs.pop(0)
    else:
        cols = refs.pop(0)
        before = None if first else refs.pop(0)
        del refs[:after_other]
        after = [refs.pop(0) for _ in range(len(spans) + 1)] if last else refs.pop(0)
    stacked, rows, high, low = refs
    half = full // 2
    if first == "features":
        for k, source in enumerate(sources):
            cols[:, k * width : (k + 1) * width] = point_features(source[...], inverse, False)
    step = 2 if len(spans) % 2 == 0 else 1
    sums = [None] * len(spans)
    for n in range(count):
        a, b = parts_of(blocks[n][:full] * 4.0, 2)
        stacked[:full] = a
        stacked[full:] = b
        rows[...] = point_features(blocks[n][full : full + 3], inverse, True)
        for k in range(0, len(spans), step):
            evaluate(rows, 0, cols[:, spans[k] * width : (spans[k] + step) * width], high, low, 0, 128)
            coarse, fine = product(stacked[...], full, high[...], low[...])
            total = coarse[:full] + coarse[full:] + fine
            at = slice(k * width, (k + step) * width)
            if n:
                total = sums[k] + total
            elif not first:
                total = before[:, skip + at.start : skip + at.stop] + total
            sums[k] = total
            if n < count - 1:
                continue
            if not last:
                after[:, at] = total
                continue
            mine = jnp.where(core[0] == 0, total[:half], total[half:])
            for i in range(step):
                after[k + i][...] = mine[:, i * width : (i + 1) * width]
            after[-1][:, at] = jnp.where(core[0] == 0, total[half:], total[:half])


def keep_kernel(inverse, start, row_points, col_points, high, low, zero, rows, cols):
    zero[...] = jnp.zeros_like(zero)
    rows[...] = point_features(row_points[:, start : start + rows.shape[1]], inverse, True)
    cols[...] = point_features(col_points[...], inverse, False)
    count, width = rows.shape[1], math.gcd(cols.shape[1], 1024)
    sub = math.gcd(count, 256)

    def tile(which, carry):
        at = pl.ds(pl.multiple_of(which * width, width), width)
        wide = cols[:, at]
        for row in range(0, count, sub):
            square = lax.dot_general(
                rows[:, row : row + sub], wide, (((0,), (0,)), ((), ())), preferred_element_type=F32
            )
            value = quarter_wendland(square)
            rounded = value.astype(BF16)
            high[row : row + sub, at] = rounded
            low[row : row + sub, at] = (value - rounded.astype(F32)).astype(BF16)
        return carry

    lax.fori_loop(0, cols.shape[1] // width, tile, 0)


def step_kernel(half, start, count, spans, with_sums, first, last, *refs):
    refs = list(refs)
    blocks = [refs.pop(0) for _ in range(count)]
    high, low = refs.pop(0), refs.pop(0)
    before = None if first else refs.pop(0)
    del refs[:1]
    stacked, outs = refs[-1], refs[:-1]
    size = blocks[0].shape[1]
    upper = half + (ONES if with_sums else 0)
    for k in range(count):
        a, b = parts_of(blocks[k][...] * 4.0, 2)
        stacked[:half, k * size : (k + 1) * size] = a
        stacked[upper:, k * size : (k + 1) * size] = b
    if with_sums:
        stacked[half:upper, :] = jnp.full((ONES, stacked.shape[1]), 4.0, BF16)
    step = 2 if len(spans) % 2 == 0 else 1
    along = slice(start * size, (start + count) * size)
    for k in range(0, len(spans), step):
        span = slice(spans[k] * size, (spans[k] + step) * size)
        coarse, fine = product(stacked[...], upper, high[along, span], low[along, span])
        total = coarse[:half] + coarse[upper:] + fine[:half]
        sums = coarse[half : half + 8] + fine[half : half + 8] if with_sums else None
        if not first:
            total = before[:half, span] + total
            sums = before[half:, span] + sums if with_sums else None
        if not last:
            outs[0][:half, span] = total
            if with_sums:
                outs[0][half:, span] = sums
            continue
        for i in range(step):
            at = slice(i * size, (i + 1) * size)
            outs[k + i][:half] = total[:, at]
            if with_sums:
                outs[k + i][half:] = sums[:, at]


def again_kernel(inverse, half, peers, with_sums, *refs):
    blocks, row_points, col_points = refs[:peers], refs[peers], refs[peers + 1]
    outs = refs[peers + 2 : 2 * peers + 2]
    stacked, rows, cols, high, low = refs[2 * peers + 2 :]
    count = blocks[0].shape[1]
    upper = half + (ONES if with_sums else 0)
    rows[...] = point_features(row_points[...], inverse, True)
    cols[...] = point_features(col_points[...], inverse, False)
    if with_sums:
        stacked[half:upper, :] = jnp.full((ONES, count), 4.0, BF16)
    for k in range(peers):
        a, b = parts_of(blocks[k][...] * 4.0, 2)
        stacked[:half] = a
        stacked[upper:] = b
        for j in range(peers):
            mine = rows[:, k * count : (k + 1) * count]
            evaluate(mine, 0, cols[:, j * count : (j + 1) * count], high, low, 0, 128)
            coarse, fine = product(stacked[...], upper, high[...], low[...])
            total = coarse[:half] + coarse[upper:] + fine[:half]
            outs[j][:half] = total if k == 0 else outs[j][:half] + total
            if with_sums:
                sums = coarse[half : half + 8] + fine[half : half + 8]
                outs[j][half:] = sums if k == 0 else outs[j][half:] + sums


def vmem(count):
    return [pl.BlockSpec(memory_space=pltpu.VMEM)] * count


def params():
    return pltpu.CompilerParams(vmem_limit_bytes=24 << 20)


def cost(rows, half, weight=1):
    return pl.CostEstimate(flops=rows * half * weight, bytes_accessed=half, transcendentals=0)


def per_device(vol_grad, vol_coords, ctrl_coords):
    tgt, src = lax.axis_size("tgt"), lax.axis_size("src")
    chips = src // 2
    peers = tgt
    if chips != tgt or src % 2 or tgt & (tgt - 1):
        raise ValueError("unsupported mesh")
    half = vol_grad.shape[0] // 2
    volume, owned = vol_grad.shape[1], ctrl_coords.shape[1]
    overall = owned * tgt * src
    radius = (3.0 * neighbours / (4.0 * math.pi * overall)) ** (1.0 / 3.0)
    inverse = 1.0 / radius
    core = lax.axis_index("src") % 2
    first_core = core == 0

    sibling = [(i, i ^ 1) for i in range(src)]

    def moved(flips):
        return [
            ((t * chips + c) * 2 + r, ((t ^ flips[r][0]) * chips + (c ^ flips[r][1])) * 2 + r)
            for t in range(tgt)
            for c in range(chips)
            for r in range(2)
        ]

    along_src = [moved(((0, k), (0, k))) for k in range(peers)]
    along_tgt = [moved(((k, 0), (k, 0))) for k in range(peers)]
    gather_pairs = [moved(((0, k), (k, 0))) for k in range(peers)]
    sum_pairs = [moved(((k, 0), (0, k))) for k in range(peers)]

    def exchange(value, pairs):
        return lax.ppermute(value, ("tgt", "src"), pairs)

    def ordered(mine, other, axis):
        return jnp.where(
            first_core, jnp.concatenate([mine, other], axis=axis), jnp.concatenate([other, mine], axis=axis)
        )

    block = jnp.concatenate(
        [
            vol_grad,
            vol_coords,
            jnp.pad(ctrl_coords, ((0, 0), (0, volume - owned))),
            jnp.zeros((COORDS - 6, volume), F32),
        ],
        axis=0,
    )
    got = lax.ppermute(ctrl_coords, "src", sibling)
    block, got = lax.optimization_barrier((block, got))
    ctrl = ordered(ctrl_coords, got, 1)
    blocks = [block] + [exchange(block, along_src[k]) for k in range(1, peers)]
    tgt_ctrl = [ctrl] + [exchange(ctrl, along_tgt[k]) for k in range(1, peers)]

    width, full = 2 * owned, 2 * half
    total_width = peers * width
    core_of = jnp.reshape(core, (1,)).astype(jnp.int32)
    scalar = [pl.BlockSpec(memory_space=pltpu.SMEM)]
    anywhere = [pl.BlockSpec(memory_space=pl.ANY)]

    def pull(which, spans, cols, before, last, skip=0, other=(), weight=1):
        first = before is None
        step = 2 if len(spans) % 2 == 0 else 1
        if last:
            shapes = [jax.ShapeDtypeStruct((half, width), F32)] * len(spans)
            shapes.append(jax.ShapeDtypeStruct((half, len(spans) * width), F32))
        else:
            shapes = [pltpu.VMEM((full, len(spans) * width), F32)]
        inputs = [core_of, *[blocks[k] for k in which]]
        if cols is None:
            first = "features"
            shapes = [pltpu.VMEM((FEATURES, len(spans) * width), BF16)] + shapes
            inputs += [tgt_ctrl[k] for k in spans]
        else:
            inputs.append(pltpu.with_memory_space_constraint(cols, pltpu.VMEM))
        if not first:
            inputs.append(pltpu.with_memory_space_constraint(before, pltpu.VMEM))
        in_specs = scalar + vmem(len(inputs) - 1) + anywhere * len(other)
        inputs += other
        extra = len(spans) if cols is None else len(other)
        return pl.pallas_call(
            functools.partial(
                pull_kernel, inverse, full, width, len(which), [within[k] for k in spans], skip, first, last, extra
            ),
            out_shape=shapes,
            in_specs=in_specs,
            out_specs=vmem(len(shapes)),
            scratch_shapes=[
                pltpu.VMEM((2 * full, volume), BF16),
                pltpu.VMEM((FEATURES, volume), BF16),
                pltpu.VMEM((volume, step * width), BF16),
                pltpu.VMEM((volume, step * width), BF16),
            ],
            compiler_params=params(),
            cost_estimate=cost(len(which) * volume, full, weight),
        )(*inputs)

    near, far = list(range(peers // 2)), list(range(peers // 2, peers))
    within = {k: k - half_of[0] for half_of in (near, far) for k in half_of}
    near_cols, near_sofar = pull([0], near, None, None, False)
    far_cols, far_sofar = pull([0], far, None, None, False)
    sums = [None] * peers
    arriving = list(range(1, peers))

    def swapped(other, pieces=1):
        rows = half // pieces
        return [lax.ppermute(other[i * rows : (i + 1) * rows], "src", sibling) for i in range(pieces)]

    def added(spans, mine, other):
        other = jnp.concatenate(other, axis=0)
        for i, k in enumerate(spans):
            sums[k] = mine[i] + other[:, i * width : (i + 1) * width]

    if peers > 2:
        (far_sofar,) = pull(arriving[:1], far, far_cols, far_sofar, False, weight=8 * width)
    *mine, other = pull(arriving[1:] or arriving, far, far_cols, far_sofar, True, weight=8 * width)
    late, _ = lax.optimization_barrier((blocks[1:], other))
    theirs = jnp.concatenate([b[full + 3 : full + 6, :owned] for b in late], axis=1)
    others = lax.ppermute(theirs, "src", sibling)
    src_points = [ctrl]
    for k in range(peers - 1):
        at = slice(k * owned, (k + 1) * owned)
        src_points.append(ordered(theirs[:, at], others[:, at], 1))
    src_points = jnp.concatenate(src_points, axis=1)
    tgt_points = jnp.concatenate(tgt_ctrl, axis=1)
    row_points = jnp.where(first_core, src_points, tgt_points)
    col_points = jnp.where(first_core, tgt_points, src_points)
    given = swapped(other)
    if near[1:]:
        *near_mine, other = pull(arriving, near[1:], near_cols, near_sofar, True, width, [other], 4 * width)
        near_given = swapped(other)
    added(far, mine, given)
    *mine, other = pull(
        arriving, near[:1], near_cols, near_sofar, True, 0, [sums[k] for k in far]
    )
    if near[1:]:
        near_given, mine, other = lax.optimization_barrier((near_given, mine, other))
        added(near[1:], near_mine, near_given)
    added(near[:1], mine, swapped(other))

    def summed(values):
        order = [peers // 2] + [k for k in range(1, peers) if k != peers // 2]
        got = {k: exchange(values[k], sum_pairs[k]) for k in order}
        total = values[0]
        for k in order:
            total = total + got[k]
        return total

    kept = (peers * width) ** 2 * 4 <= KEPT_BYTES
    pullback = sums[0]

    def keep(start, count):
        return pl.pallas_call(
            functools.partial(keep_kernel, inverse, start * width),
            out_shape=[pltpu.VMEM((count * width, total_width), BF16)] * 2
            + [jax.ShapeDtypeStruct((1, width), F32)],
            in_specs=vmem(2),
            out_specs=vmem(3),
            scratch_shapes=[pltpu.VMEM((FEATURES, count * width), BF16), pltpu.VMEM((FEATURES, total_width), BF16)],
            compiler_params=params(),
            cost_estimate=cost(total_width, half),
        )(row_points, col_points)

    if kept:
        *early, zero = keep(0, peers - 1)
        *final, after_final = keep(peers - 1, 1)
        pullback = pullback + zero

    def step(these, part, start, spans, before, with_sums, last, other):
        out_rows = half + (8 if with_sums else 0)
        if last:
            shapes = [jax.ShapeDtypeStruct((out_rows, width), F32)] * len(spans)
        else:
            shapes = [pltpu.VMEM((out_rows, total_width), F32)]
        inputs = these + [pltpu.with_memory_space_constraint(value, pltpu.VMEM) for value in part]
        if before is not None:
            inputs.append(pltpu.with_memory_space_constraint(before, pltpu.VMEM))
        upper = half + (ONES if with_sums else 0)
        return pl.pallas_call(
            functools.partial(
                step_kernel, half, start, len(these), spans, with_sums, before is None, last
            ),
            out_shape=shapes,
            in_specs=vmem(len(inputs)) + anywhere,
            out_specs=vmem(len(shapes)),
            scratch_shapes=[pltpu.VMEM((upper + half, len(these) * width), BF16)],
            compiler_params=params(),
            cost_estimate=cost(total_width, half),
        )(*inputs, other)

    got = {k: exchange(sums[k], along_tgt[k]) for k in range(peers - 1, 0, -1)}
    for value in got.values():
        pullback = pullback + value

    iterate = pullback
    for sweep in range(STEPS):
        arrived = [iterate] + [exchange(iterate, gather_pairs[k]) for k in range(1, peers)]
        with_sums = sweep == 0
        if kept:
            spans = near + far
            (sofar,) = step(arrived[:1], early, 0, spans, None, with_sums, False, after_final)
            if peers > 2:
                (sofar,) = step(arrived[1:-1], early, 1, spans, sofar, with_sums, False, after_final)
            products = step(arrived[-1:], final, 0, spans, sofar, with_sums, True, after_final)
        else:
            upper = half + (ONES if with_sums else 0)
            out_rows = half + (8 if with_sums else 0)
            products = pl.pallas_call(
                functools.partial(again_kernel, inverse, half, peers, with_sums),
                out_shape=[jax.ShapeDtypeStruct((out_rows, width), F32)] * peers,
                in_specs=vmem(peers + 2),
                out_specs=vmem(peers),
                scratch_shapes=[
                    pltpu.VMEM((upper + half, width), BF16),
                    pltpu.VMEM((FEATURES, peers * width), BF16),
                    pltpu.VMEM((FEATURES, peers * width), BF16),
                    pltpu.VMEM((width, width), BF16),
                    pltpu.VMEM((width, width), BF16),
                ],
                compiler_params=params(),
                cost_estimate=cost(total_width, half),
            )(*arrived, row_points, col_points)
        total = summed(products)
        if with_sums:
            scaling = 1.0 / (total[half : half + 1] + ridge_term)
        iterate = iterate + omegas[sweep] * scaling * (pullback - total[:half] - iterate)

    own = jnp.where(first_core, iterate[:, :owned], iterate[:, owned:])
    theirs = jnp.where(first_core, iterate[:, owned:], iterate[:, :owned])
    back = lax.ppermute(theirs, "src", sibling)
    return jnp.where(
        first_core, jnp.concatenate([own, back], axis=0), jnp.concatenate([back, own], axis=0)
    )


def solution(mesh):
    placed = (P(None, ("tgt", "src")), P(None, ("tgt", "src")), P(None, ("tgt", "src")))
    return jax.shard_map(
        per_device, mesh=mesh, in_specs=placed, out_specs=P(None, ("tgt", "src")), check_vma=False
    )
```

```python
import functools
import math

import jax
import jax.numpy as jnp
from jax import lax
from jax.experimental import pallas as pl
from jax.experimental.pallas import tpu as pltpu
from jax.sharding import PartitionSpec as P

STEPS = 2
COORDS = 8
FEATURES = 32
ONES = 16
KEPT_BYTES = 20 << 20

neighbours = 64.0
ridge_term = 1.0
omegas = [1.0 / (0.55 + 0.45 * math.cos(math.pi * (2 * k + 1) / 4.0)) for k in range(2)]

BF16 = jnp.bfloat16
F32 = jnp.float32


def parts_of(value, count):
    terms = []
    for _ in range(count):
        term = value.astype(BF16)
        terms.append(term)
        value = value - term.astype(F32)
    return terms


def point_features(points, inverse, as_rows):
    scaled = (points - 0.5) * inverse
    axes = [scaled[d : d + 1] for d in range(3)]
    norm = parts_of(axes[0] * axes[0] + axes[1] * axes[1] + axes[2] * axes[2], 3)
    one = jnp.ones_like(norm[0])
    found = []
    for axis in axes:
        if as_rows:
            a, b, c = parts_of(-2.0 * axis, 3)
            found += [a, a, b, b, a, c]
        else:
            a, b, c = parts_of(axis, 3)
            found += [a, b, a, b, c, a]
    found += norm + [one] * 3 if as_rows else [one] * 3 + norm
    found += [jnp.zeros_like(one)] * (FEATURES - len(found))
    return jnp.concatenate([f.astype(F32) for f in found], axis=0).astype(BF16)


def quarter_wendland(square):
    square = jnp.minimum(jnp.maximum(square, 1e-12), 1.0)
    distance = square * lax.rsqrt(square)
    falloff = 1.0 - distance
    falloff = falloff * falloff
    return (falloff * falloff) * (distance + 0.25)


def evaluate(rows, row_start, cols, high, low, high_start, sub):
    count, width = rows.shape[1], cols.shape[1]
    for at in range(0, count, sub):
        square = lax.dot_general(
            rows[:, at : at + sub], cols, (((0,), (0,)), ((), ())), preferred_element_type=F32
        )
        value = quarter_wendland(square)
        rounded = value.astype(BF16)
        high[row_start + at : row_start + at + sub, high_start : high_start + width] = rounded
        low[row_start + at : row_start + at + sub, high_start : high_start + width] = (
            value - rounded.astype(F32)
        ).astype(BF16)


def product(stacked, half, high, low):
    coarse = jnp.dot(stacked, high, preferred_element_type=F32)
    fine = jnp.dot(stacked[:half], low, preferred_element_type=F32)
    return coarse, fine


def pull_kernel(inverse, full, width, count, spans, skip, first, last, after_other, *refs):
    refs = list(refs)
    core = refs.pop(0)
    blocks = [refs.pop(0) for _ in range(count)]
    if first == "features":
        sources = [refs.pop(0) for _ in range(after_other)]
        cols, after = refs.pop(0), refs.pop(0)
    else:
        cols = refs.pop(0)
        before = None if first else refs.pop(0)
        del refs[:after_other]
        after = [refs.pop(0) for _ in range(len(spans) + 1)] if last else refs.pop(0)
    stacked, rows, high, low = refs
    half = full // 2
    if first == "features":
        for k, source in enumerate(sources):
            cols[:, k * width : (k + 1) * width] = point_features(source[...], inverse, False)
    step = 2 if len(spans) % 2 == 0 else 1
    length = blocks[0].shape[1]
    for n in range(count):
        along = slice(n * length, (n + 1) * length)
        a, b = parts_of(blocks[n][:full] * 4.0, 2)
        stacked[:full, along] = a
        stacked[full:, along] = b
        rows[:, along] = point_features(blocks[n][full : full + 3], inverse, True)
    for k in range(0, len(spans), step):
        evaluate(rows, 0, cols[:, spans[k] * width : (spans[k] + step) * width], high, low, 0, 128)
        coarse, fine = product(stacked[...], full, high[...], low[...])
        total = coarse[:full] + coarse[full:] + fine
        at = slice(k * width, (k + step) * width)
        if not first:
            total = before[:, skip + at.start : skip + at.stop] + total
        if not last:
            after[:, at] = total
            continue
        mine = jnp.where(core[0] == 0, total[:half], total[half:])
        for i in range(step):
            after[k + i][...] = mine[:, i * width : (i + 1) * width]
        after[-1][:, at] = jnp.where(core[0] == 0, total[half:], total[:half])


def keep_kernel(inverse, start, row_points, col_points, high, low, zero, rows, cols):
    zero[...] = jnp.zeros_like(zero)
    rows[...] = point_features(row_points[:, start : start + rows.shape[1]], inverse, True)
    cols[...] = point_features(col_points[...], inverse, False)
    count, width = rows.shape[1], math.gcd(cols.shape[1], 1024)
    sub = math.gcd(count, 256)

    def tile(which, carry):
        at = pl.ds(pl.multiple_of(which * width, width), width)
        wide = cols[:, at]
        for row in range(0, count, sub):
            square = lax.dot_general(
                rows[:, row : row + sub], wide, (((0,), (0,)), ((), ())), preferred_element_type=F32
            )
            value = quarter_wendland(square)
            rounded = value.astype(BF16)
            high[row : row + sub, at] = rounded
            low[row : row + sub, at] = (value - rounded.astype(F32)).astype(BF16)
        return carry

    lax.fori_loop(0, cols.shape[1] // width, tile, 0)


def step_kernel(half, start, count, spans, with_sums, first, last, *refs):
    refs = list(refs)
    blocks = [refs.pop(0) for _ in range(count)]
    high, low = refs.pop(0), refs.pop(0)
    before = None if first else refs.pop(0)
    del refs[:1]
    stacked, outs = refs[-1], refs[:-1]
    size = blocks[0].shape[1]
    upper = half + (ONES if with_sums else 0)
    for k in range(count):
        a, b = parts_of(blocks[k][...] * 4.0, 2)
        stacked[:half, k * size : (k + 1) * size] = a
        stacked[upper:, k * size : (k + 1) * size] = b
    if with_sums:
        stacked[half:upper, :] = jnp.full((ONES, stacked.shape[1]), 4.0, BF16)
    step = 2 if len(spans) % 2 == 0 else 1
    along = slice(start * size, (start + count) * size)
    for k in range(0, len(spans), step):
        span = slice(spans[k] * size, (spans[k] + step) * size)
        coarse, fine = product(stacked[...], upper, high[along, span], low[along, span])
        total = coarse[:half] + coarse[upper:] + fine[:half]
        sums = coarse[half : half + 8] + fine[half : half + 8] if with_sums else None
        if not first:
            total = before[:half, span] + total
            sums = before[half:, span] + sums if with_sums else None
        if not last:
            outs[0][:half, span] = total
            if with_sums:
                outs[0][half:, span] = sums
            continue
        for i in range(step):
            at = slice(i * size, (i + 1) * size)
            outs[k + i][:half] = total[:, at]
            if with_sums:
                outs[k + i][half:] = sums[:, at]


def again_kernel(inverse, half, peers, with_sums, *refs):
    blocks, row_points, col_points = refs[:peers], refs[peers], refs[peers + 1]
    outs = refs[peers + 2 : 2 * peers + 2]
    stacked, rows, cols, high, low = refs[2 * peers + 2 :]
    count = blocks[0].shape[1]
    upper = half + (ONES if with_sums else 0)
    rows[...] = point_features(row_points[...], inverse, True)
    cols[...] = point_features(col_points[...], inverse, False)
    if with_sums:
        stacked[half:upper, :] = jnp.full((ONES, count), 4.0, BF16)
    for k in range(peers):
        a, b = parts_of(blocks[k][...] * 4.0, 2)
        stacked[:half] = a
        stacked[upper:] = b
        for j in range(peers):
            mine = rows[:, k * count : (k + 1) * count]
            evaluate(mine, 0, cols[:, j * count : (j + 1) * count], high, low, 0, 128)
            coarse, fine = product(stacked[...], upper, high[...], low[...])
            total = coarse[:half] + coarse[upper:] + fine[:half]
            outs[j][:half] = total if k == 0 else outs[j][:half] + total
            if with_sums:
                sums = coarse[half : half + 8] + fine[half : half + 8]
                outs[j][half:] = sums if k == 0 else outs[j][half:] + sums


def vmem(count):
    return [pl.BlockSpec(memory_space=pltpu.VMEM)] * count


def params():
    return pltpu.CompilerParams(vmem_limit_bytes=24 << 20)


def cost(rows, half, weight=1):
    return pl.CostEstimate(flops=rows * half * weight, bytes_accessed=half, transcendentals=0)


def per_device(vol_grad, vol_coords, ctrl_coords):
    tgt, src = lax.axis_size("tgt"), lax.axis_size("src")
    chips = src // 2
    peers = tgt
    if chips != tgt or src % 2 or tgt & (tgt - 1):
        raise ValueError("unsupported mesh")
    half = vol_grad.shape[0] // 2
    volume, owned = vol_grad.shape[1], ctrl_coords.shape[1]
    overall = owned * tgt * src
    radius = (3.0 * neighbours / (4.0 * math.pi * overall)) ** (1.0 / 3.0)
    inverse = 1.0 / radius
    core = lax.axis_index("src") % 2
    first_core = core == 0

    sibling = [(i, i ^ 1) for i in range(src)]

    def moved(flips):
        return [
            ((t * chips + c) * 2 + r, ((t ^ flips[r][0]) * chips + (c ^ flips[r][1])) * 2 + r)
            for t in range(tgt)
            for c in range(chips)
            for r in range(2)
        ]

    along_src = [moved(((0, k), (0, k))) for k in range(peers)]
    along_tgt = [moved(((k, 0), (k, 0))) for k in range(peers)]
    gather_pairs = [moved(((0, k), (k, 0))) for k in range(peers)]
    sum_pairs = [moved(((k, 0), (0, k))) for k in range(peers)]

    def exchange(value, pairs):
        return lax.ppermute(value, ("tgt", "src"), pairs)

    def ordered(mine, other, axis):
        return jnp.where(
            first_core, jnp.concatenate([mine, other], axis=axis), jnp.concatenate([other, mine], axis=axis)
        )

    block = jnp.concatenate(
        [
            vol_grad,
            vol_coords,
            jnp.pad(ctrl_coords, ((0, 0), (0, volume - owned))),
            jnp.zeros((COORDS - 6, volume), F32),
        ],
        axis=0,
    )
    got = lax.ppermute(ctrl_coords, "src", sibling)
    block, got = lax.optimization_barrier((block, got))
    ctrl = ordered(ctrl_coords, got, 1)
    blocks = [block] + [exchange(block, along_src[k]) for k in range(1, peers)]
    tgt_ctrl = [ctrl] + [exchange(ctrl, along_tgt[k]) for k in range(1, peers)]

    width, full = 2 * owned, 2 * half
    total_width = peers * width
    core_of = jnp.reshape(core, (1,)).astype(jnp.int32)
    scalar = [pl.BlockSpec(memory_space=pltpu.SMEM)]
    anywhere = [pl.BlockSpec(memory_space=pl.ANY)]

    def pull(which, spans, cols, before, last, skip=0, other=(), weight=1):
        first = before is None
        step = 2 if len(spans) % 2 == 0 else 1
        if last:
            shapes = [jax.ShapeDtypeStruct((half, width), F32)] * len(spans)
            shapes.append(jax.ShapeDtypeStruct((half, len(spans) * width), F32))
        else:
            shapes = [pltpu.VMEM((full, len(spans) * width), F32)]
        inputs = [core_of, *[blocks[k] for k in which]]
        if cols is None:
            first = "features"
            shapes = [pltpu.VMEM((FEATURES, len(spans) * width), BF16)] + shapes
            inputs += [tgt_ctrl[k] for k in spans]
        else:
            inputs.append(pltpu.with_memory_space_constraint(cols, pltpu.VMEM))
        if not first:
            inputs.append(pltpu.with_memory_space_constraint(before, pltpu.VMEM))
        in_specs = scalar + vmem(len(inputs) - 1) + anywhere * len(other)
        inputs += other
        extra = len(spans) if cols is None else len(other)
        return pl.pallas_call(
            functools.partial(
                pull_kernel, inverse, full, width, len(which), [within[k] for k in spans], skip, first, last, extra
            ),
            out_shape=shapes,
            in_specs=in_specs,
            out_specs=vmem(len(shapes)),
            scratch_shapes=[
                pltpu.VMEM((2 * full, len(which) * volume), BF16),
                pltpu.VMEM((FEATURES, len(which) * volume), BF16),
                pltpu.VMEM((len(which) * volume, step * width), BF16),
                pltpu.VMEM((len(which) * volume, step * width), BF16),
            ],
            compiler_params=params(),
            cost_estimate=cost(len(which) * volume, full, weight),
        )(*inputs)

    near, far = list(range(peers // 2)), list(range(peers // 2, peers))
    within = {k: k - half_of[0] for half_of in (near, far) for k in half_of}
    near_cols, near_sofar = pull([0], near, None, None, False)
    far_cols, far_sofar = pull([0], far, None, None, False)
    sums = [None] * peers
    arriving = list(range(1, peers))

    def swapped(other, pieces=1):
        rows = half // pieces
        return [lax.ppermute(other[i * rows : (i + 1) * rows], "src", sibling) for i in range(pieces)]

    def added(spans, mine, other):
        other = jnp.concatenate(other, axis=0)
        for i, k in enumerate(spans):
            sums[k] = mine[i] + other[:, i * width : (i + 1) * width]

    if peers > 2:
        (far_sofar,) = pull(arriving[:1], far, far_cols, far_sofar, False, weight=8 * width)
    *mine, other = pull(arriving[1:] or arriving, far, far_cols, far_sofar, True, weight=8 * width)
    late, _ = lax.optimization_barrier((blocks[1:], other))
    theirs = jnp.concatenate([b[full + 3 : full + 6, :owned] for b in late], axis=1)
    others = lax.ppermute(theirs, "src", sibling)
    src_points = [ctrl]
    for k in range(peers - 1):
        at = slice(k * owned, (k + 1) * owned)
        src_points.append(ordered(theirs[:, at], others[:, at], 1))
    src_points = jnp.concatenate(src_points, axis=1)
    tgt_points = jnp.concatenate(tgt_ctrl, axis=1)
    row_points = jnp.where(first_core, src_points, tgt_points)
    col_points = jnp.where(first_core, tgt_points, src_points)
    given = swapped(other)
    if near[1:]:
        *near_mine, other = pull(arriving, near[1:], near_cols, near_sofar, True, width, [other], 4 * width)
        near_given = swapped(other)
    added(far, mine, given)
    *mine, other = pull(
        arriving, near[:1], near_cols, near_sofar, True, 0, [sums[k] for k in far]
    )
    if near[1:]:
        near_given, mine, other = lax.optimization_barrier((near_given, mine, other))
        added(near[1:], near_mine, near_given)
    added(near[:1], mine, swapped(other))

    def summed(values):
        order = [peers // 2] + [k for k in range(1, peers) if k != peers // 2]
        got = {k: exchange(values[k], sum_pairs[k]) for k in order}
        total = values[0]
        for k in order:
            total = total + got[k]
        return total

    kept = (peers * width) ** 2 * 4 <= KEPT_BYTES
    pullback = sums[0]

    def keep(start, count):
        return pl.pallas_call(
            functools.partial(keep_kernel, inverse, start * width),
            out_shape=[pltpu.VMEM((count * width, total_width), BF16)] * 2
            + [jax.ShapeDtypeStruct((1, width), F32)],
            in_specs=vmem(2),
            out_specs=vmem(3),
            scratch_shapes=[pltpu.VMEM((FEATURES, count * width), BF16), pltpu.VMEM((FEATURES, total_width), BF16)],
            compiler_params=params(),
            cost_estimate=cost(total_width, half),
        )(row_points, col_points)

    if kept:
        *early, zero = keep(0, peers - 1)
        *final, after_final = keep(peers - 1, 1)
        pullback = pullback + zero

    def step(these, part, start, spans, before, with_sums, last, other):
        out_rows = half + (8 if with_sums else 0)
        if last:
            shapes = [jax.ShapeDtypeStruct((out_rows, width), F32)] * len(spans)
        else:
            shapes = [pltpu.VMEM((out_rows, total_width), F32)]
        inputs = these + [pltpu.with_memory_space_constraint(value, pltpu.VMEM) for value in part]
        if before is not None:
            inputs.append(pltpu.with_memory_space_constraint(before, pltpu.VMEM))
        upper = half + (ONES if with_sums else 0)
        return pl.pallas_call(
            functools.partial(
                step_kernel, half, start, len(these), spans, with_sums, before is None, last
            ),
            out_shape=shapes,
            in_specs=vmem(len(inputs)) + anywhere,
            out_specs=vmem(len(shapes)),
            scratch_shapes=[pltpu.VMEM((upper + half, len(these) * width), BF16)],
            compiler_params=params(),
            cost_estimate=cost(total_width, half),
        )(*inputs, other)

    got = {k: exchange(sums[k], along_tgt[k]) for k in range(peers - 1, 0, -1)}
    for value in got.values():
        pullback = pullback + value

    iterate = pullback
    for sweep in range(STEPS):
        arrived = [iterate] + [exchange(iterate, gather_pairs[k]) for k in range(1, peers)]
        with_sums = sweep == 0
        if kept:
            spans = near + far
            (sofar,) = step(arrived[:1], early, 0, spans, None, with_sums, False, after_final)
            if peers > 2:
                (sofar,) = step(arrived[1:-1], early, 1, spans, sofar, with_sums, False, after_final)
            products = step(arrived[-1:], final, 0, spans, sofar, with_sums, True, after_final)
        else:
            upper = half + (ONES if with_sums else 0)
            out_rows = half + (8 if with_sums else 0)
            products = pl.pallas_call(
                functools.partial(again_kernel, inverse, half, peers, with_sums),
                out_shape=[jax.ShapeDtypeStruct((out_rows, width), F32)] * peers,
                in_specs=vmem(peers + 2),
                out_specs=vmem(peers),
                scratch_shapes=[
                    pltpu.VMEM((upper + half, width), BF16),
                    pltpu.VMEM((FEATURES, peers * width), BF16),
                    pltpu.VMEM((FEATURES, peers * width), BF16),
                    pltpu.VMEM((width, width), BF16),
                    pltpu.VMEM((width, width), BF16),
                ],
                compiler_params=params(),
                cost_estimate=cost(total_width, half),
            )(*arrived, row_points, col_points)
        total = summed(products)
        if with_sums:
            scaling = 1.0 / (total[half : half + 1] + ridge_term)
        iterate = iterate + omegas[sweep] * scaling * (pullback - total[:half] - iterate)

    own = jnp.where(first_core, iterate[:, :owned], iterate[:, owned:])
    theirs = jnp.where(first_core, iterate[:, owned:], iterate[:, :owned])
    back = lax.ppermute(theirs, "src", sibling)
    return jnp.where(
        first_core, jnp.concatenate([own, back], axis=0), jnp.concatenate([back, own], axis=0)
    )


def solution(mesh):
    placed = (P(None, ("tgt", "src")), P(None, ("tgt", "src")), P(None, ("tgt", "src")))
    return jax.shard_map(
        per_device, mesh=mesh, in_specs=placed, out_specs=P(None, ("tgt", "src")), check_vma=False
    )
```

```python
import functools
import math

import jax
import jax.numpy as jnp
from jax import lax
from jax.experimental import pallas as pl
from jax.experimental.pallas import tpu as pltpu
from jax.sharding import PartitionSpec as P

STEPS = 2
COORDS = 8
FEATURES = 32
ONES = 16
KEPT_BYTES = 20 << 20

neighbours = 64.0
ridge_term = 1.0
omegas = [1.0 / (0.55 + 0.45 * math.cos(math.pi * (2 * k + 1) / 4.0)) for k in range(2)]

BF16 = jnp.bfloat16
F32 = jnp.float32


def parts_of(value, count):
    terms = []
    for _ in range(count):
        term = value.astype(BF16)
        terms.append(term)
        value = value - term.astype(F32)
    return terms


def point_features(points, inverse, as_rows):
    scaled = (points - 0.5) * inverse
    axes = [scaled[d : d + 1] for d in range(3)]
    norm = parts_of(axes[0] * axes[0] + axes[1] * axes[1] + axes[2] * axes[2], 3)
    one = jnp.ones_like(norm[0])
    found = []
    for axis in axes:
        if as_rows:
            a, b, c = parts_of(-2.0 * axis, 3)
            found += [a, a, b, b, a, c]
        else:
            a, b, c = parts_of(axis, 3)
            found += [a, b, a, b, c, a]
    found += norm + [one] * 3 if as_rows else [one] * 3 + norm
    found += [jnp.zeros_like(one)] * (FEATURES - len(found))
    return jnp.concatenate([f.astype(F32) for f in found], axis=0).astype(BF16)


def quarter_wendland(square):
    square = jnp.minimum(jnp.maximum(square, 1e-12), 1.0)
    distance = square * lax.rsqrt(square)
    falloff = 1.0 - distance
    falloff = falloff * falloff
    return (falloff * falloff) * (distance + 0.25)


def evaluate(rows, row_start, cols, high, low, high_start, sub):
    count, width = rows.shape[1], cols.shape[1]
    for at in range(0, count, sub):
        square = lax.dot_general(
            rows[:, at : at + sub], cols, (((0,), (0,)), ((), ())), preferred_element_type=F32
        )
        value = quarter_wendland(square)
        rounded = value.astype(BF16)
        high[row_start + at : row_start + at + sub, high_start : high_start + width] = rounded
        low[row_start + at : row_start + at + sub, high_start : high_start + width] = (
            value - rounded.astype(F32)
        ).astype(BF16)


def product(stacked, half, high, low):
    coarse = jnp.dot(stacked, high, preferred_element_type=F32)
    fine = jnp.dot(stacked[:half], low, preferred_element_type=F32)
    return coarse, fine


def pull_kernel(inverse, full, width, count, spans, skip, first, last, after_other, *refs):
    refs = list(refs)
    core = refs.pop(0)
    blocks = [refs.pop(0) for _ in range(count)]
    if first == "features":
        sources = [refs.pop(0) for _ in range(after_other)]
        cols, after = refs.pop(0), refs.pop(0)
    else:
        cols = refs.pop(0)
        before = None if first else refs.pop(0)
        del refs[:after_other]
        after = [refs.pop(0) for _ in range(len(spans) + 1)] if last else refs.pop(0)
    stacked, rows, high, low = refs
    half = full // 2
    if first == "features":
        for k, source in enumerate(sources):
            cols[:, k * width : (k + 1) * width] = point_features(source[...], inverse, False)
    step = 2 if len(spans) % 2 == 0 else 1
    sums = [None] * len(spans)
    for n in range(count):
        a, b = parts_of(blocks[n][:full] * 4.0, 2)
        stacked[:full] = a
        stacked[full:] = b
        rows[...] = point_features(blocks[n][full : full + 3], inverse, True)
        for k in range(0, len(spans), step):
            evaluate(rows, 0, cols[:, spans[k] * width : (spans[k] + step) * width], high, low, 0, 128)
            coarse, fine = product(stacked[...], full, high[...], low[...])
            total = coarse[:full] + coarse[full:] + fine
            at = slice(k * width, (k + step) * width)
            if n:
                total = sums[k] + total
            elif not first:
                total = before[:, skip + at.start : skip + at.stop] + total
            sums[k] = total
            if n < count - 1:
                continue
            if not last:
                after[:, at] = total
                continue
            mine = jnp.where(core[0] == 0, total[:half], total[half:])
            for i in range(step):
                after[k + i][...] = mine[:, i * width : (i + 1) * width]
            after[-1][:, at] = jnp.where(core[0] == 0, total[half:], total[:half])


def keep_kernel(inverse, start, row_points, col_points, high, low, zero, rows, cols):
    zero[...] = jnp.zeros_like(zero)
    rows[...] = point_features(row_points[:, start : start + rows.shape[1]], inverse, True)
    cols[...] = point_features(col_points[...], inverse, False)
    count, width = rows.shape[1], math.gcd(cols.shape[1], 1024)
    sub = math.gcd(count, 256)

    def tile(which, carry):
        at = pl.ds(pl.multiple_of(which * width, width), width)
        wide = cols[:, at]
        for row in range(0, count, sub):
            square = lax.dot_general(
                rows[:, row : row + sub], wide, (((0,), (0,)), ((), ())), preferred_element_type=F32
            )
            value = quarter_wendland(square)
            rounded = value.astype(BF16)
            high[row : row + sub, at] = rounded
            low[row : row + sub, at] = (value - rounded.astype(F32)).astype(BF16)
        return carry

    lax.fori_loop(0, cols.shape[1] // width, tile, 0)


def step_kernel(half, start, count, spans, with_sums, first, last, *refs):
    refs = list(refs)
    blocks = [refs.pop(0) for _ in range(count)]
    high, low = refs.pop(0), refs.pop(0)
    before = None if first else refs.pop(0)
    del refs[:1]
    stacked, outs = refs[-1], refs[:-1]
    size = blocks[0].shape[1]
    upper = half + (ONES if with_sums else 0)
    for k in range(count):
        a, b = parts_of(blocks[k][...] * 4.0, 2)
        stacked[:half, k * size : (k + 1) * size] = a
        stacked[upper:, k * size : (k + 1) * size] = b
    if with_sums:
        stacked[half:upper, :] = jnp.full((ONES, stacked.shape[1]), 4.0, BF16)
    step = 2 if len(spans) % 2 == 0 else 1
    along = slice(start * size, (start + count) * size)
    for k in range(0, len(spans), step):
        span = slice(spans[k] * size, (spans[k] + step) * size)
        coarse, fine = product(stacked[...], upper, high[along, span], low[along, span])
        total = coarse[:half] + coarse[upper:] + fine[:half]
        sums = coarse[half : half + 8] + fine[half : half + 8] if with_sums else None
        if not first:
            total = before[:half, span] + total
            sums = before[half:, span] + sums if with_sums else None
        if not last:
            outs[0][:half, span] = total
            if with_sums:
                outs[0][half:, span] = sums
            continue
        for i in range(step):
            at = slice(i * size, (i + 1) * size)
            outs[k + i][:half] = total[:, at]
            if with_sums:
                outs[k + i][half:] = sums[:, at]


def again_kernel(inverse, half, peers, with_sums, *refs):
    blocks, row_points, col_points = refs[:peers], refs[peers], refs[peers + 1]
    outs = refs[peers + 2 : 2 * peers + 2]
    stacked, rows, cols, high, low = refs[2 * peers + 2 :]
    count = blocks[0].shape[1]
    upper = half + (ONES if with_sums else 0)
    rows[...] = point_features(row_points[...], inverse, True)
    cols[...] = point_features(col_points[...], inverse, False)
    if with_sums:
        stacked[half:upper, :] = jnp.full((ONES, count), 4.0, BF16)
    for k in range(peers):
        a, b = parts_of(blocks[k][...] * 4.0, 2)
        stacked[:half] = a
        stacked[upper:] = b
        for j in range(peers):
            mine = rows[:, k * count : (k + 1) * count]
            evaluate(mine, 0, cols[:, j * count : (j + 1) * count], high, low, 0, 128)
            coarse, fine = product(stacked[...], upper, high[...], low[...])
            total = coarse[:half] + coarse[upper:] + fine[:half]
            outs[j][:half] = total if k == 0 else outs[j][:half] + total
            if with_sums:
                sums = coarse[half : half + 8] + fine[half : half + 8]
                outs[j][half:] = sums if k == 0 else outs[j][half:] + sums


def vmem(count):
    return [pl.BlockSpec(memory_space=pltpu.VMEM)] * count


def params():
    return pltpu.CompilerParams(vmem_limit_bytes=24 << 20)


def cost(rows, half, weight=1):
    return pl.CostEstimate(flops=rows * half * weight, bytes_accessed=half, transcendentals=0)


def per_device(vol_grad, vol_coords, ctrl_coords):
    tgt, src = lax.axis_size("tgt"), lax.axis_size("src")
    chips = src // 2
    peers = tgt
    if chips != tgt or src % 2 or tgt & (tgt - 1):
        raise ValueError("unsupported mesh")
    half = vol_grad.shape[0] // 2
    volume, owned = vol_grad.shape[1], ctrl_coords.shape[1]
    overall = owned * tgt * src
    radius = (3.0 * neighbours / (4.0 * math.pi * overall)) ** (1.0 / 3.0)
    inverse = 1.0 / radius
    core = lax.axis_index("src") % 2
    first_core = core == 0

    sibling = [(i, i ^ 1) for i in range(src)]

    def moved(flips):
        return [
            ((t * chips + c) * 2 + r, ((t ^ flips[r][0]) * chips + (c ^ flips[r][1])) * 2 + r)
            for t in range(tgt)
            for c in range(chips)
            for r in range(2)
        ]

    along_src = [moved(((0, k), (0, k))) for k in range(peers)]
    along_tgt = [moved(((k, 0), (k, 0))) for k in range(peers)]
    gather_pairs = [moved(((0, k), (k, 0))) for k in range(peers)]
    sum_pairs = [moved(((k, 0), (0, k))) for k in range(peers)]

    def exchange(value, pairs):
        return lax.ppermute(value, ("tgt", "src"), pairs)

    def ordered(mine, other, axis):
        return jnp.where(
            first_core, jnp.concatenate([mine, other], axis=axis), jnp.concatenate([other, mine], axis=axis)
        )

    block = jnp.concatenate(
        [
            vol_grad,
            vol_coords,
            jnp.pad(ctrl_coords, ((0, 0), (0, volume - owned))),
            jnp.zeros((COORDS - 6, volume), F32),
        ],
        axis=0,
    )
    got = lax.ppermute(ctrl_coords, "src", sibling)
    block, got = lax.optimization_barrier((block, got))
    ctrl = ordered(ctrl_coords, got, 1)
    blocks = [block] + [exchange(block, along_src[k]) for k in range(1, peers)]
    tgt_ctrl = [ctrl] + [exchange(ctrl, along_tgt[k]) for k in range(peers - 1, 0, -1)][::-1]

    width, full = 2 * owned, 2 * half
    total_width = peers * width
    core_of = jnp.reshape(core, (1,)).astype(jnp.int32)
    scalar = [pl.BlockSpec(memory_space=pltpu.SMEM)]
    anywhere = [pl.BlockSpec(memory_space=pl.ANY)]

    def pull(which, spans, cols, before, last, skip=0, other=(), weight=1):
        first = before is None
        step = 2 if len(spans) % 2 == 0 else 1
        if last:
            shapes = [jax.ShapeDtypeStruct((half, width), F32)] * len(spans)
            shapes.append(jax.ShapeDtypeStruct((half, len(spans) * width), F32))
        else:
            shapes = [pltpu.VMEM((full, len(spans) * width), F32)]
        inputs = [core_of, *[blocks[k] for k in which]]
        if cols is None:
            first = "features"
            shapes = [pltpu.VMEM((FEATURES, len(spans) * width), BF16)] + shapes
            inputs += [tgt_ctrl[k] for k in spans]
        else:
            inputs.append(pltpu.with_memory_space_constraint(cols, pltpu.VMEM))
        if not first:
            inputs.append(pltpu.with_memory_space_constraint(before, pltpu.VMEM))
        in_specs = scalar + vmem(len(inputs) - 1) + anywhere * len(other)
        inputs += other
        extra = len(spans) if cols is None else len(other)
        return pl.pallas_call(
            functools.partial(
                pull_kernel, inverse, full, width, len(which), [within[k] for k in spans], skip, first, last, extra
            ),
            out_shape=shapes,
            in_specs=in_specs,
            out_specs=vmem(len(shapes)),
            scratch_shapes=[
                pltpu.VMEM((2 * full, volume), BF16),
                pltpu.VMEM((FEATURES, volume), BF16),
                pltpu.VMEM((volume, step * width), BF16),
                pltpu.VMEM((volume, step * width), BF16),
            ],
            compiler_params=params(),
            cost_estimate=cost(len(which) * volume, full, weight),
        )(*inputs)

    near, far = list(range(peers // 2)), list(range(peers // 2, peers))
    within = {k: k - half_of[0] for half_of in (near, far) for k in half_of}
    near_cols, near_sofar = pull([0], near, None, None, False)
    far_cols, far_sofar = pull([0], far, None, None, False)
    sums = [None] * peers
    arriving = list(range(1, peers))

    def swapped(other, pieces=1):
        rows = half // pieces
        return [lax.ppermute(other[i * rows : (i + 1) * rows], "src", sibling) for i in range(pieces)]

    def added(spans, mine, other):
        other = jnp.concatenate(other, axis=0)
        for i, k in enumerate(spans):
            sums[k] = mine[i] + other[:, i * width : (i + 1) * width]

    if peers > 2:
        (far_sofar,) = pull(arriving[:1], far, far_cols, far_sofar, False, weight=8 * width)
    *mine, other = pull(arriving[1:] or arriving, far, far_cols, far_sofar, True, weight=8 * width)
    late, _ = lax.optimization_barrier((blocks[1:], other))
    theirs = jnp.concatenate([b[full + 3 : full + 6, :owned] for b in late], axis=1)
    others = lax.ppermute(theirs, "src", sibling)
    src_points = [ctrl]
    for k in range(peers - 1):
        at = slice(k * owned, (k + 1) * owned)
        src_points.append(ordered(theirs[:, at], others[:, at], 1))
    src_points = jnp.concatenate(src_points, axis=1)
    tgt_points = jnp.concatenate(tgt_ctrl, axis=1)
    row_points = jnp.where(first_core, src_points, tgt_points)
    col_points = jnp.where(first_core, tgt_points, src_points)
    given = swapped(other)
    if near[1:]:
        *near_mine, other = pull(arriving, near[1:], near_cols, near_sofar, True, width, [other], 4 * width)
        near_given = swapped(other)
    added(far, mine, given)
    *mine, other = pull(
        arriving, near[:1], near_cols, near_sofar, True, 0, [sums[k] for k in far]
    )
    if near[1:]:
        near_given, mine, other = lax.optimization_barrier((near_given, mine, other))
        added(near[1:], near_mine, near_given)
    added(near[:1], mine, swapped(other))

    def summed(values):
        order = [peers // 2] + [k for k in range(1, peers) if k != peers // 2]
        got = {k: exchange(values[k], sum_pairs[k]) for k in order}
        total = values[0]
        for k in order:
            total = total + got[k]
        return total

    kept = (peers * width) ** 2 * 4 <= KEPT_BYTES
    pullback = sums[0]

    def keep(start, count):
        return pl.pallas_call(
            functools.partial(keep_kernel, inverse, start * width),
            out_shape=[pltpu.VMEM((count * width, total_width), BF16)] * 2
            + [jax.ShapeDtypeStruct((1, width), F32)],
            in_specs=vmem(2),
            out_specs=vmem(3),
            scratch_shapes=[pltpu.VMEM((FEATURES, count * width), BF16), pltpu.VMEM((FEATURES, total_width), BF16)],
            compiler_params=params(),
            cost_estimate=cost(total_width, half),
        )(row_points, col_points)

    if kept:
        *early, zero = keep(0, peers - 1)
        *final, after_final = keep(peers - 1, 1)
        pullback = pullback + zero

    def step(these, part, start, spans, before, with_sums, last, other):
        out_rows = half + (8 if with_sums else 0)
        if last:
            shapes = [jax.ShapeDtypeStruct((out_rows, width), F32)] * len(spans)
        else:
            shapes = [pltpu.VMEM((out_rows, total_width), F32)]
        inputs = these + [pltpu.with_memory_space_constraint(value, pltpu.VMEM) for value in part]
        if before is not None:
            inputs.append(pltpu.with_memory_space_constraint(before, pltpu.VMEM))
        upper = half + (ONES if with_sums else 0)
        return pl.pallas_call(
            functools.partial(
                step_kernel, half, start, len(these), spans, with_sums, before is None, last
            ),
            out_shape=shapes,
            in_specs=vmem(len(inputs)) + anywhere,
            out_specs=vmem(len(shapes)),
            scratch_shapes=[pltpu.VMEM((upper + half, len(these) * width), BF16)],
            compiler_params=params(),
            cost_estimate=cost(total_width, half),
        )(*inputs, other)

    got = {k: exchange(sums[k], along_tgt[k]) for k in range(peers - 1, 0, -1)}
    for value in got.values():
        pullback = pullback + value

    iterate = pullback
    for sweep in range(STEPS):
        arrived = [iterate] + [exchange(iterate, gather_pairs[k]) for k in range(1, peers)]
        with_sums = sweep == 0
        if kept:
            spans = near + far
            (sofar,) = step(arrived[:1], early, 0, spans, None, with_sums, False, after_final)
            if peers > 2:
                (sofar,) = step(arrived[1:-1], early, 1, spans, sofar, with_sums, False, after_final)
            products = step(arrived[-1:], final, 0, spans, sofar, with_sums, True, after_final)
        else:
            upper = half + (ONES if with_sums else 0)
            out_rows = half + (8 if with_sums else 0)
            products = pl.pallas_call(
                functools.partial(again_kernel, inverse, half, peers, with_sums),
                out_shape=[jax.ShapeDtypeStruct((out_rows, width), F32)] * peers,
                in_specs=vmem(peers + 2),
                out_specs=vmem(peers),
                scratch_shapes=[
                    pltpu.VMEM((upper + half, width), BF16),
                    pltpu.VMEM((FEATURES, peers * width), BF16),
                    pltpu.VMEM((FEATURES, peers * width), BF16),
                    pltpu.VMEM((width, width), BF16),
                    pltpu.VMEM((width, width), BF16),
                ],
                compiler_params=params(),
                cost_estimate=cost(total_width, half),
            )(*arrived, row_points, col_points)
        total = summed(products)
        if with_sums:
            scaling = 1.0 / (total[half : half + 1] + ridge_term)
        iterate = iterate + omegas[sweep] * scaling * (pullback - total[:half] - iterate)

    own = jnp.where(first_core, iterate[:, :owned], iterate[:, owned:])
    theirs = jnp.where(first_core, iterate[:, owned:], iterate[:, :owned])
    back = lax.ppermute(theirs, "src", sibling)
    return lax.dynamic_update_slice(jnp.concatenate([own, own], axis=0), back, (jnp.where(first_core, half, 0), 0))


def solution(mesh):
    placed = (P(None, ("tgt", "src")), P(None, ("tgt", "src")), P(None, ("tgt", "src")))
    return jax.shard_map(
        per_device, mesh=mesh, in_specs=placed, out_specs=P(None, ("tgt", "src")), check_vma=False
    )
```
